32 devices in a mesh: group: 8 (over y, x, core), band: 4 (over z).
Axes of the slice: x: 2, y: 2, z: 4, core: 2. Of those that a mesh axis runs over, the one named last changes fastest.
Arguments:
- station_rows: int32 [8, 96, 128], P('group', 'band'), may hold values from 0 to 3
- station_lons: int32 [8, 96, 128], P('group', 'band'), may hold values from 0 to 1439
- station_obs: float32 [8, 96, 128], P('group', 'band'), may hold values from -6 to 6
- station_live: int32 [8, 96, 128], P('group', 'band'), may hold values 0 or 1
- block_band: int32 [8, 96, 1], P('group', 'band'), may hold values from 0 to 3; in each aligned block of 24 rows (0 to 23, 24 to 47, ..., all dimensions but the last counted through in order) at most 12 rows name the same one
- truth_field: float32 [8, 16, 1440], P('group', 'band'), may hold values from -6 to 6
- length_scales: float32 [4], replicated, may hold values from 1.5 to 6
- w_in: bfloat16 [3, 3, 32, 8], replicated, may hold values from -0.75 to 0.75
- w_down: bfloat16 [4, 4, 32, 32], replicated, may hold values from -0.25 to 0.25
- w_mid: bfloat16 [3, 3, 32, 32], replicated, may hold values from -0.375 to 0.375
- w_up: bfloat16 [3, 3, 32, 64], replicated, may hold values from -0.25 to 0.25
- w_head: bfloat16 [2, 32], replicated, may hold values from -1 to 1
Outputs:
- mean_field: float32 [8, 16, 1440], P('group', 'band')
- grad_in: float32 [3, 3, 32, 8], replicated
- grad_down: float32 [4, 4, 32, 32], replicated
- grad_mid: float32 [3, 3, 32, 32], replicated
- grad_up: float32 [3, 3, 32, 64], replicated
- grad_head: float32 [2, 32], replicated
The draws below stay inside these ranges and needn't reach their ends.
Inputs may be any that keep to these rules, and one draw needn't show every extreme that they name: `block_band`: among the 24 blocks of one device no band is named by more than 12 blocks, and that number is reached.
All inputs are finite; a program needn't handle non-finite values. No bound on the sum of `station_live` on one device may be relied on, other than what follows from the above.
Results may differ from the reference program's by a relative error of at most 0.0025.
The reference program's roundings to bfloat16 on the way count: a program that leaves them out, or rounds other values in their place, can miss the bound.
Values may be sent and summed in bfloat16 or wider, within the bound.
No kernel may reach another device: no remote copies, remote signals or barrier semaphores. Data moves between devices by JAX's collectives and lax.ppermute only.
A program may use at most 64 MiB of HBM per device.

```python
import math
import jax
import jax.numpy as jnp
import numpy as np
from jax import lax

C = 32
SCALES = 4
LON = 1440
BS = 128
ROWS_DEV = 4
NBLK = 24
SC = 8
CAP = 12
DATES = 8
LAT = 16
BLOCKS = 96
N_BAND = 4


def plant(drawn, stream_key, smallest, top_value):
    dims = drawn.shape
    index_at = [jax.random.randint(jax.random.fold_in(stream_key, axis), (), 0, dims[axis]) for axis in range(len(dims))]
    drawn = drawn.at[tuple(index_at)].set(smallest)
    longest = dims.index(max(dims))
    index_at[longest] = (index_at[longest] + 1) % dims[longest]
    return drawn.at[tuple(index_at)].set(top_value)


def block_scale(rng, extent, cuts, least, largest):
    gain, own = 1.0, jax.random.fold_in(rng, 6)
    for position, shards_of in cuts:
        steps = jnp.exp(jax.random.uniform(jax.random.fold_in(own, position), (shards_of,), jnp.float32, least / len(cuts), largest / len(cuts)))
        gain = gain * jnp.repeat(steps, extent[position] // shards_of).reshape([-1 if axis == position else 1 for axis in range(len(extent))])
    return gain


def deal_out(stream_key, own, number, rows, count, top, reach, slope):
    sequence = jax.random.permutation(stream_key, count)
    packed, ordinary = portions_of(count, rows * top, reach, slope, True), portions_of(count, rows * top, reach, slope, False)
    places = jnp.arange(count)

    def named(lengths, turn):
        used = int((lengths > 0).sum())
        fixed = max(1, used // 4)
        passed = fixed + (places - fixed + turn * (used - fixed)) % max(1, count - fixed)
        return jnp.zeros((count,), jnp.int32).at[sequence[jnp.where(places < fixed, places, passed)]].set(jnp.asarray(lengths, jnp.int32))

    lengths = jnp.where(number % 4 == 0, named(packed, number // 4), named(ordinary, number - number // 4 - 1))
    mixed = jax.random.permutation(jax.random.fold_in(own, 3), count)
    donor, sink = mixed[0:count // 2 * 2:2], mixed[1:count // 2 * 2:2]
    room = jnp.minimum(lengths[donor] - 1, reach - lengths[sink]) // 2
    room = jnp.where((donor == sequence[0]) | (sink == sequence[0]) | (lengths[sink] == 0), 0, jnp.maximum(room, 0))
    passed = jax.random.randint(jax.random.fold_in(own, 4), (count // 2,), 0, 1 << 20) % (room + 1)
    lengths = lengths.at[donor].add(-passed).at[sink].add(passed)
    items = jnp.searchsorted(jnp.cumsum(lengths), jnp.arange(rows * top), side="right").astype(jnp.int32)
    grid = items.reshape(top, rows).T
    grid = grid[jax.random.permutation(jax.random.fold_in(own, 1), rows)]
    turn = jax.random.randint(jax.random.fold_in(own, 2), (rows, 1), 0, top)
    return jnp.take_along_axis(grid, (jnp.arange(top)[None, :] + turn) % top, axis=1)


def portions_of(count, total, reach, skew, full):
    loads = [(1 << 20) // math.isqrt(grade ** skew) + 1 for grade in range(1, count + 1)]
    largest = reach if full else min(reach, max(-(-total // count), total * loads[0] // sum(loads)))
    least = 1 if total - largest >= count - 1 else 0
    holding, rest = [largest] + [least] * (count - 1), total - largest - least * (count - 1)
    while rest > 0:
        candidates = [i for i in range(1, count) if holding[i] < largest] or [i for i in range(1, count) if holding[i] < reach]
        whole, left = sum([loads[i] for i in candidates]), rest
        for i in candidates:
            extra = min(reach - holding[i], max(1, left * loads[i] // whole), rest)
            holding[i] = holding[i] + extra
            rest = rest - extra
    return np.array(holding)


def scatter_about(rng, dims, scale, most, split=(), held_as=jnp.bfloat16):
    values = scale * jax.random.normal(rng, dims, jnp.float32)
    if split:
        values = values * block_scale(rng, dims, split, -0.22, 0.18)
    return jnp.clip(values, -most, most).astype(held_as)


def setup_inputs(seed: int = 0) -> dict:
    arg_keys = jax.random.split(jax.random.key(seed), 13)
    station_rows = plant(jax.random.randint(arg_keys[0], (DATES, BLOCKS, BS), 0, ROWS_DEV), jax.random.fold_in(arg_keys[0], 1), 0, ROWS_DEV - 1).astype(jnp.int32)
    station_lons = plant(jax.random.randint(arg_keys[1], (DATES, BLOCKS, BS), 0, LON), jax.random.fold_in(arg_keys[1], 1), 0, LON - 1).astype(jnp.int32)
    station_obs = scatter_about(arg_keys[2], (DATES, BLOCKS, BS), 1.0, 6.0, ((0, 8), (1, 4)), jnp.float32)
    station_live = plant((jax.random.randint(arg_keys[3], (DATES, BLOCKS, BS), 0, 4) < 3).astype(jnp.int32), jax.random.fold_in(arg_keys[3], 1), 0, 1)
    block_band_keys = jax.random.split(jax.random.fold_in(arg_keys[4], 1), DATES * BLOCKS // NBLK)
    block_band_turns = jax.random.permutation(jax.random.fold_in(arg_keys[4], 3), DATES * BLOCKS // NBLK)
    block_band = jax.vmap(lambda own, number: deal_out(jax.random.fold_in(arg_keys[4], 2), own, number, NBLK, N_BAND, 1, CAP, 2))(block_band_keys, block_band_turns).reshape((DATES, BLOCKS, 1))
    truth_field = scatter_about(arg_keys[5], (DATES, LAT, LON), 1.0, 6.0, ((0, 8), (1, 4)), jnp.float32)
    length_scales = jnp.clip(jnp.exp(jax.random.uniform(arg_keys[6], (SCALES,), jnp.float32, math.log(1.5), math.log(6.0))), 1.5, 6.0)
    w_in = scatter_about(arg_keys[7], (3, 3, C, SC), (9 * SC) ** -0.5, 0.75)
    w_down = scatter_about(arg_keys[8], (4, 4, C, C), (16 * C) ** -0.5, 0.25)
    w_mid = scatter_about(arg_keys[9], (3, 3, C, C), (9 * C) ** -0.5, 0.375)
    w_up = scatter_about(arg_keys[10], (3, 3, C, 2 * C), (18 * C) ** -0.5, 0.25)
    w_head = scatter_about(arg_keys[11], (2, C), C ** -0.5, 1.0)
    return {"station_rows": station_rows, "station_lons": station_lons, "station_obs": station_obs, "station_live": station_live, "block_band": block_band, "truth_field": truth_field, "length_scales": length_scales, "w_in": w_in, "w_down": w_down, "w_mid": w_mid, "w_up": w_up, "w_head": w_head}


PHASES = (((1, 0), (3, -1)), ((0, 1), (2, 0)))


def widen(values):
    return lax.optimization_barrier(values).astype(jnp.float32)


def contract(form, first, second):
    return jnp.einsum(form, widen(first), widen(second))


def wrap_cols(values, left_count, right_count):
    total_cols = values.shape[-1]
    return jnp.concatenate([values[..., total_cols - left_count:], values, values[..., :right_count]], axis=-1)


def zero_rims(values, margin):
    zeros = jnp.zeros((margin,) + values.shape[1:], values.dtype)
    return jnp.concatenate([zeros, values, zeros], axis=0)


def conv_three(padded, weight, dilate):
    row_count = padded.shape[0] - 2 * dilate
    widened = wrap_cols(padded, dilate, dilate)
    col_count = widened.shape[-1] - 2 * dilate
    summed = None
    for tap_row in range(3):
        for tap_col in range(3):
            window = widened[tap_row * dilate:tap_row * dilate + row_count, :, tap_col * dilate:tap_col * dilate + col_count]
            contrib = contract("oc,rcl->rol", weight[tap_row, tap_col], window)
            summed = contrib if summed is None else summed + contrib
    return summed


def grad_three(padded, grad_out, dilate):
    row_count = grad_out.shape[0]
    col_count = grad_out.shape[-1]
    widened = wrap_cols(padded, dilate, dilate)
    pieces = []
    for tap_row in range(3):
        for tap_col in range(3):
            window = widened[tap_row * dilate:tap_row * dilate + row_count, :, tap_col * dilate:tap_col * dilate + col_count]
            pieces.append(contract("rol,rcl->oc", grad_out, window))
    stacked = jnp.stack(pieces)
    return stacked.reshape((3, 3) + stacked.shape[1:])


def conv_down(padded, weight):
    row_count = (padded.shape[0] - 2) // 2
    widened = wrap_cols(padded, 1, 1)
    col_count = (widened.shape[-1] - 2) // 2
    summed = None
    for tap_row in range(4):
        for tap_col in range(4):
            window = widened[tap_row:tap_row + 2 * row_count - 1:2, :, tap_col:tap_col + 2 * col_count - 1:2]
            contrib = contract("oc,rcl->rol", weight[tap_row, tap_col], window)
            summed = contrib if summed is None else summed + contrib
    return summed


def grad_strided(padded, grad_out):
    row_count = grad_out.shape[0]
    col_count = grad_out.shape[-1]
    widened = wrap_cols(padded, 1, 1)
    pieces = []
    for tap_row in range(4):
        for tap_col in range(4):
            window = widened[tap_row:tap_row + 2 * row_count - 1:2, :, tap_col:tap_col + 2 * col_count - 1:2]
            pieces.append(contract("rol,rcl->oc", grad_out, window))
    stacked = jnp.stack(pieces)
    return stacked.reshape((4, 4) + stacked.shape[1:])


def back_down(grad_pad, weight):
    row_count = grad_pad.shape[0] - 2
    widened = wrap_cols(grad_pad, 1, 1)
    col_count = widened.shape[-1] - 2
    phase_rows = []
    for phase_row in range(2):
        phase_cols = []
        for phase_col in range(2):
            summed = None
            for tap_row, shift_row in PHASES[phase_row]:
                for tap_col, shift_col in PHASES[phase_col]:
                    window = widened[1 + shift_row:1 + shift_row + row_count, :, 1 + shift_col:1 + shift_col + col_count]
                    contrib = contract("oc,rol->rcl", weight[tap_row, tap_col], window)
                    summed = contrib if summed is None else summed + contrib
            phase_cols.append(summed)
        phase_rows.append(jnp.stack(phase_cols, axis=-1))
    stacked = jnp.stack(phase_rows, axis=1)
    return stacked.reshape(2 * row_count, stacked.shape[2], 2 * col_count)


def flipped(weight):
    return jnp.transpose(weight[::-1, ::-1], (0, 1, 3, 2))


def silu_slope(pre_act):
    squash = jax.nn.sigmoid(pre_act)
    return squash * (1.0 + pre_act * (1.0 - squash))


def station_terms(row_pos, lon_pos, observed, alive, length_scales, row_count, lon_count):
    grid_rows = jnp.arange(row_count).astype(jnp.float32)
    grid_lons = jnp.arange(lon_count).astype(jnp.float32)
    row_gap = grid_rows[None, None, :] - row_pos[:, :, None]
    lon_gap = jnp.abs(grid_lons[None, None, :] - lon_pos[:, :, None])
    lon_gap = jnp.minimum(lon_gap, lon_count - lon_gap)
    factors = jnp.stack([alive, alive * observed], axis=2)
    per_scale = []
    for scale_index in range(length_scales.shape[0]):
        spread = length_scales[scale_index]
        left_side = (factors[:, :, :, None] * jnp.exp(-0.5 * (row_gap / spread) ** 2)[:, :, None, :]).astype(jnp.bfloat16)
        right_side = jnp.exp(-0.5 * (lon_gap / spread) ** 2).astype(jnp.bfloat16)
        per_scale.append(contract("bskr,bsl->brkl", left_side, right_side))
    stacked = jnp.stack(per_scale, axis=2)
    return stacked.reshape(stacked.shape[0], row_count, 2 * length_scales.shape[0], lon_count)


def features_of(sums):
    density = sums[:, 0::2]
    signal = sums[:, 1::2]
    scaled = jnp.stack([density / (1.0 + density), signal / (1.0 + density)], axis=2)
    return scaled.reshape(sums.shape).astype(jnp.bfloat16)


def network(features, truth_date, w_in, w_down, w_mid, w_up, w_head, cell_count):
    feat_pad = zero_rims(features, 1)
    pre_one = conv_three(feat_pad, w_in, 1)
    hidden_one = jax.nn.silu(pre_one).astype(jnp.bfloat16)
    one_pad = zero_rims(hidden_one, 1)
    pre_two = conv_down(one_pad, w_down)
    hidden_two = jax.nn.silu(pre_two).astype(jnp.bfloat16)
    two_pad = zero_rims(hidden_two, 2)
    pre_three = conv_three(two_pad, w_mid, 2)
    hidden_three = jax.nn.silu(pre_three).astype(jnp.bfloat16)
    upsampled = jnp.repeat(jnp.repeat(hidden_three, 2, axis=0), 2, axis=2)
    joined_pad = jnp.concatenate([zero_rims(upsampled, 1), one_pad], axis=1)
    pre_four = conv_three(joined_pad, w_up, 1)
    hidden_four = jax.nn.silu(pre_four).astype(jnp.bfloat16)
    head_out = contract("kc,rcl->rkl", w_head, hidden_four)
    mean_field = head_out[:, 0]
    raw_spread = head_out[:, 1]
    noise_scale = 0.1 + jax.nn.softplus(raw_spread)
    scaled_error = (mean_field - truth_date) / noise_scale
    grad_mean = scaled_error / (noise_scale * cell_count)
    grad_raw = (1.0 - scaled_error * scaled_error) / (noise_scale * cell_count) * jax.nn.sigmoid(raw_spread)
    grad_head_out = jnp.stack([grad_mean, grad_raw], axis=1).astype(jnp.bfloat16)
    grad_head = contract("rkl,rcl->kc", grad_head_out, hidden_four)
    grad_hidden_four = contract("kc,rkl->rcl", w_head, grad_head_out)
    grad_pre_four = (grad_hidden_four * silu_slope(pre_four)).astype(jnp.bfloat16)
    grad_up = grad_three(joined_pad, grad_pre_four, 1)
    grad_joined = conv_three(zero_rims(grad_pre_four, 1), flipped(w_up), 1).astype(jnp.bfloat16)
    grad_joined = lax.optimization_barrier(grad_joined)
    channels = hidden_one.shape[1]
    grad_upsampled = grad_joined[:, :channels].astype(jnp.float32)
    half_rows = hidden_three.shape[0]
    half_cols = hidden_three.shape[2]
    grad_hidden_three = grad_upsampled.reshape(half_rows, 2, channels, half_cols, 2).sum(axis=(1, 4))
    grad_pre_three = (grad_hidden_three * silu_slope(pre_three)).astype(jnp.bfloat16)
    grad_mid = grad_three(two_pad, grad_pre_three, 2)
    grad_hidden_two = conv_three(zero_rims(grad_pre_three, 2), flipped(w_mid), 2)
    grad_pre_two = (grad_hidden_two * silu_slope(pre_two)).astype(jnp.bfloat16)
    grad_down = grad_strided(one_pad, grad_pre_two)
    grad_hidden_one = back_down(zero_rims(grad_pre_two, 1), w_down) + grad_joined[:, channels:].astype(jnp.float32)
    grad_pre_one = (grad_hidden_one * silu_slope(pre_one)).astype(jnp.bfloat16)
    grad_in = grad_three(feat_pad, grad_pre_one, 1)
    return mean_field, (grad_in, grad_down, grad_mid, grad_up, grad_head)


def date_sums(rows_date, lons_date, obs_date, live_date, band_date, length_scales):
    def one_group(running, group):
        rows_group, lons_group, obs_group, live_group, band_group = group
        terms = station_terms(rows_group.astype(jnp.float32), lons_group.astype(jnp.float32), obs_group, live_group.astype(jnp.float32), length_scales, ROWS_DEV, LON)
        running = running + jax.ops.segment_sum(terms, band_group, num_segments=N_BAND)
        return running, None

    grouped = tuple(values.reshape((N_BAND, NBLK) + values.shape[1:]) for values in (rows_date, lons_date, obs_date, live_date, band_date[:, 0]))
    initial = jnp.zeros((N_BAND, ROWS_DEV, SC, LON), jnp.float32)
    running, _ = lax.scan(one_group, initial, grouped)
    return running.reshape(LAT, SC, LON)


def reference(station_rows, station_lons, station_obs, station_live, block_band, truth_field, length_scales, w_in, w_down, w_mid, w_up, w_head):
    def one_date(inputs):
        rows_date, lons_date, obs_date, live_date, band_date, truth_date = inputs
        sums = date_sums(rows_date, lons_date, obs_date, live_date, band_date, length_scales)
        features = features_of(sums)
        return network(features, truth_date, w_in, w_down, w_mid, w_up, w_head, float(LAT * LON))

    mean_fields, grads = lax.map(one_date, (station_rows, station_lons, station_obs, station_live, block_band, truth_field))
    return (mean_fields, jnp.sum(grads[0], axis=0), jnp.sum(grads[1], axis=0), jnp.sum(grads[2], axis=0), jnp.sum(grads[3], axis=0), jnp.sum(grads[4], axis=0))
```

```python
import functools

import jax
import jax.numpy as jnp
import numpy as np
from jax import lax
from jax.experimental import pallas as pl
from jax.experimental.pallas import tpu as pltpu
from jax.sharding import PartitionSpec as P

LANES = 128
HALO = 64
REACH = 128
ROWS_BAND = 4
FAR = -1.0e6
F32 = jnp.float32
BF16 = jnp.bfloat16


def looped(count, step, body):
    step = min(step, count)
    if count == step:
        for index in range(count):
            body(index)
    else:

        def turn(outer, carry):
            for inner in range(step):
                body(outer * step + inner)
            return carry

        lax.fori_loop(0, count // step, turn, 0)


def dot(first, second):
    return jnp.dot(first, second, preferred_element_type=F32)


def dot_lanes(first, second):
    return lax.dot_general(first, second, (((1,), (1,)), ((), ())), preferred_element_type=F32)


def rolled(values, shift):
    width = values.shape[-1]
    return pltpu.roll(values, shift % width, values.ndim - 1)


def four_shifts(even, odd):
    return jnp.concatenate([rolled(odd, 1), even, odd, rolled(even, -1)], axis=0)


def three_shifts(values, width):
    return jnp.concatenate([rolled(values, width), values, rolled(values, -width)], axis=0)


def sigmoid(values):
    return 1.0 / (1.0 + jnp.exp(-values))


def silu(values):
    return values * sigmoid(values)


def silu_slope(values):
    squash = sigmoid(values)
    return squash * (1.0 + values * (1.0 - squash))


def split_three(values):
    high = values.astype(BF16).astype(F32)
    rest = values - high
    middle = rest.astype(BF16).astype(F32)
    return high, middle, rest - middle


def network_kernel(sizes, *refs):
    n_band, n_blocks, own, lon_count = sizes
    window = own + 2 * HALO
    half = window // 2
    rows = ROWS_BAND * n_band
    coarse = rows // 2
    hist_tiles = (window + 2 * REACH) // LANES
    own_tiles = own // LANES
    pays = refs[:n_band]
    (scales, w1, wd, wm, wu, wh, wht, wf, wmf, wbd) = refs[n_band : n_band + 10]
    grads_out, mean_out = refs[n_band + 10 : n_band + 12]
    (
        bands, hist, table, zf, p1, zj, p2, z2, p3, p4, h4, truth, mean_split,
        gs, gp4m, gj, gp3m, zg3, gp2m, zg2, gp1m, hi_pos, lo_pos,
        acc_up, acc_down, acc_mid, acc_in, acc_head,
    ) = refs[n_band + 12 :]

    me = lax.axis_index("band")
    cell_count = float(rows * lon_count)

    def iota(shape, dim):
        return lax.broadcasted_iota(jnp.int32, shape, dim)

    for source in range(n_band):
        pltpu.sync_copy(pays[source].at[pl.ds(3 * n_blocks, 8)], bands.at[source])

    hist[...] = jnp.zeros_like(hist)
    start = (me * own - HALO - REACH).astype(F32)
    for source in range(n_band):
        lon = pays[source][n_blocks : 2 * n_blocks]
        place = lon - start
        place = jnp.where(place < 0.0, place + lon_count, place)
        place = jnp.where(place < 0.0, place + lon_count, place)
        place = jnp.where(place >= lon_count, place - lon_count, place)
        tile = jnp.floor(place * (1.0 / LANES))
        hi_pos[source] = tile
        lo_pos[source] = place - tile * LANES

    m_index = iota((32, 1), 0)
    row_of = (m_index // 8).astype(F32)
    scale_of = (m_index % 8) // 2
    kind_of = m_index % 2
    spread = jnp.where(
        scale_of == 0, scales[0], jnp.where(scale_of == 1, scales[1], jnp.where(scale_of == 2, scales[2], scales[3]))
    )
    rate = -0.5 / (spread * spread)
    lane_iota = iota((LANES, LANES), 0).astype(F32)

    for source in range(n_band):

        def one_block(block, source=source):
            at_row = pays[source][pl.ds(block, 1), :]
            observed = pays[source][pl.ds(2 * n_blocks + block, 1), :]
            high = hi_pos[source, pl.ds(block, 1), :]
            low = lo_pos[source, pl.ds(block, 1), :]
            gap = row_of - at_row
            left = jnp.exp(gap * gap * rate) * jnp.where(kind_of == 0, 1.0, observed)
            spread_left = jnp.concatenate(
                [jnp.where(high == float(tile), left, 0.0) for tile in range(hist_tiles)], axis=0
            ).astype(BF16)
            one_hot = jnp.where(lane_iota == low, 1.0, 0.0).astype(BF16)
            band = bands[source, 0, block].astype(jnp.int32)
            hist[band] = hist[band] + dot_lanes(spread_left, one_hot)

        looped(n_blocks, 4, one_block)

    place_in = iota((4 * LANES, 2 * LANES), 0)
    place_out = iota((4 * LANES, 2 * LANES), 1)
    distance = (place_in - (REACH + 2 * (place_out % LANES) + place_out // LANES)).astype(F32)
    squared = distance * distance
    for scale in range(4):
        table[scale] = jnp.exp(squared * (-0.5 / (scales[scale] * scales[scale]))).astype(BF16)
    all_rows = 32 * n_band
    channel = iota((all_rows, 1), 0) % 8
    feats = []
    for chunk in range(half // LANES):
        tiles = [
            hist[:, (2 * chunk + t) * 32 : (2 * chunk + t + 1) * 32, :].reshape(all_rows, LANES)
            for t in range(4)
        ]
        cells = jnp.concatenate(tiles, axis=1)
        high = cells.astype(BF16)
        low = (cells - high.astype(F32)).astype(BF16)
        total = None
        for scale in range(4):
            keep = (channel // 2 == scale).astype(F32).astype(BF16)
            part = dot(high * keep, table[scale]) + dot(low * keep, table[scale])
            total = part if total is None else total + part
        below = pltpu.roll(total, 1, 0)
        density = jnp.where(channel % 2 == 0, total, below)
        feats.append(total / (1.0 + density))
    even = jnp.concatenate([f[:, :LANES] for f in feats], axis=1)
    odd = jnp.concatenate([f[:, LANES:] for f in feats], axis=1)
    odd_before = rolled(odd, 1)
    even_after = rolled(even, -1)
    for edge in (0, rows + 1):
        zf[edge] = jnp.zeros((32, half), BF16)
        zj[edge] = jnp.zeros((256, half), BF16)
        gs[edge] = jnp.zeros((128, half), BF16)
        gp4m[edge] = jnp.zeros((64, half), BF16)
        gp1m[edge] = jnp.zeros((64, half), BF16)
    for edge in (0, coarse + 1):
        zg2[edge] = jnp.zeros((96, half), BF16)
        gp2m[edge] = jnp.zeros((32, half), BF16)
    for edge in (0, coarse // 2 + 1):
        for par in range(2):
            z2[par, edge] = jnp.zeros((96, half), BF16)
            zg3[par, edge] = jnp.zeros((96, half), BF16)
            gp3m[par, edge] = jnp.zeros((32, half), BF16)
    for row in range(rows):
        pick = slice(row * 8, row * 8 + 8)
        zf[row + 1] = jnp.concatenate(
            [odd_before[pick], even[pick], odd[pick], even_after[pick]], axis=0
        ).astype(BF16)

    fine_iota = iota((2 * LANES, 2 * LANES), 0)
    part_iota = iota((2 * LANES, 2 * LANES), 1)
    parting = (fine_iota == 2 * (part_iota % LANES) + part_iota // LANES).astype(F32).astype(BF16)
    chunks = window // (2 * LANES)
    for source in range(n_band):
        at = lax.rem(me - source + n_band, n_band)
        pieces = []
        for chunk in range(2):
            if chunk < chunks:
                tiles = [
                    pays[source][pl.ds(3 * n_blocks + 8 + (me * own_tiles + 2 * chunk + t) * ROWS_BAND, ROWS_BAND), :]
                    for t in range(2)
                ]
                pieces.append(jnp.concatenate(tiles, axis=1))
            else:
                pieces.append(jnp.zeros((ROWS_BAND, 2 * LANES), F32))
        stacked = jnp.concatenate(split_three(jnp.concatenate(pieces, axis=0)) + (jnp.zeros((8, 2 * LANES), F32),), axis=0)
        parted = dot(stacked.astype(BF16), parting)
        parted = parted[0:8] + parted[8:16] + parted[16:24]
        for chunk in range(chunks):
            for phase in range(2):
                truth[at, phase * 4 : phase * 4 + 4, chunk * LANES : (chunk + 1) * LANES] = parted[
                    chunk * 4 : chunk * 4 + 4, phase * LANES : (phase + 1) * LANES
                ]

    def first(row):
        pre = dot(w1[...], zf[pl.ds(row, 3)].reshape(96, half))
        p1[row] = pre
        hidden = silu(pre)
        zj[row + 1, 128:256, :] = four_shifts(hidden[:32], hidden[32:]).astype(BF16)

    looped(rows, 4, first)

    def second(index):
        for par in range(2):
            row = 2 * index + par
            pre = dot(wd[...], zj[pl.ds(2 * row, 4), 128:256, :].reshape(512, half))
            p2[row] = pre
            z2[par, index + 1] = three_shifts(silu(pre), 2).astype(BF16)

    looped(coarse // 2, 4, second)

    def third(index):
        for par in range(2):
            row = 2 * index + par
            pre = dot(wm[...], z2[par, pl.ds(index, 3)].reshape(288, half))
            p3[row] = pre
            hidden = silu(pre)
            wide = four_shifts(hidden, hidden).astype(BF16)
            zj[2 * row + 1, 0:128, :] = wide
            zj[2 * row + 2, 0:128, :] = wide

    looped(coarse // 2, 4, third)

    def fourth(row):
        pre = dot(wu[...], zj[pl.ds(row, 3)].reshape(768, half))
        p4[row] = pre
        h4[row] = silu(pre).astype(BF16)

    looped(rows, 4, fourth)

    own_cells = jnp.clip(lon_count - me * own, 0, own) // 2
    place = iota((1, half), 1)
    mask = ((place >= HALO // 2) & (place < HALO // 2 + own_cells)).astype(F32)
    acc_head[...] = jnp.zeros_like(acc_head)

    def head(group):
        hidden = h4[pl.ds(4 * group, 4)].reshape(256, half)
        out = dot(wh[...], hidden)
        mean = out[:8]
        raw = out[8:]
        decay = jnp.exp(-jnp.abs(raw))
        noise = 0.1 + (jnp.maximum(raw, 0.0) + jnp.log1p(decay))
        error = (mean - truth[group]) / noise
        weight = 1.0 / (noise * cell_count)
        grad_mean = error * weight
        grad_raw = (1.0 - error * error) * weight * sigmoid(raw)
        grad_out = jnp.concatenate([grad_mean, grad_raw], axis=0)
        grad_bf = grad_out.astype(BF16)
        acc_head[...] += dot_lanes((grad_out * mask).astype(BF16), hidden)
        back = dot(wht[...], grad_bf)
        pre = p4[pl.ds(4 * group, 4)].reshape(256, half)
        grad = back * silu_slope(pre)
        for row in range(4):
            mine = grad[row * 64 : row * 64 + 64]
            gp4m[4 * group + row + 1] = (mine * mask).astype(BF16)
            gs[4 * group + row + 1] = four_shifts(mine[:32], mine[32:]).astype(BF16)
        parts = split_three(jnp.concatenate([mean[0:4], mean[4:8]], axis=1))
        mean_split[group] = jnp.concatenate(
            parts + (jnp.zeros((4, 2 * half), F32),), axis=0
        ).astype(BF16)

    looped(n_band, 1, head)

    target = iota((2 * half, own), 1) + HALO
    origin = iota((2 * half, own), 0)
    joining = (target == 2 * (origin % half) + origin // half).astype(F32).astype(BF16)
    joined = dot(mean_split[...].reshape(16 * n_band, 2 * half), joining)
    for band in range(n_band):
        four = joined[16 * band : 16 * band + 8] + joined[16 * band + 8 : 16 * band + 16]
        four = four[0:4] + four[4:8]
        for tile in range(own_tiles):
            mean_out[band, tile] = four[:, tile * LANES : (tile + 1) * LANES]

    def join_back(index):
        for par in range(2):
            row = 2 * index + par
            total = None
            for side in range(2):
                fine = 2 * row + side
                back = dot(wf[...], gs[pl.ds(fine, 3)].reshape(384, half)).astype(BF16)
                gj[fine] = back[64:]
                up = back[:64].astype(F32)
                part = up[:32] + up[32:]
                total = part if total is None else total + part
            grad = total * silu_slope(p3[row])
            gp3m[par, index + 1] = (grad * mask).astype(BF16)
            zg3[par, index + 1] = three_shifts(grad, 2).astype(BF16)

    looped(coarse // 2, 2, join_back)

    def mid_back(index):
        for par in range(2):
            row = 2 * index + par
            back = dot(wmf[...], zg3[par, pl.ds(index, 3)].reshape(288, half))
            grad = back * silu_slope(p2[row])
            gp2m[row + 1] = (grad * mask).astype(BF16)
            zg2[row + 1] = three_shifts(grad, 1).astype(BF16)

    looped(coarse // 2, 4, mid_back)

    def down_back(row):
        back = dot(wbd[...], zg2[pl.ds(row, 3)].reshape(288, half))
        for side in range(2):
            fine = 2 * row + side
            grad = (back[64 * side : 64 * side + 64] + gj[fine].astype(F32)) * silu_slope(p1[fine])
            gp1m[fine + 1] = (grad * mask).astype(BF16)

    looped(coarse, 4, down_back)

    acc_up[...] = jnp.zeros_like(acc_up)
    acc_down[...] = jnp.zeros_like(acc_down)
    acc_mid[...] = jnp.zeros_like(acc_mid)
    acc_in[...] = jnp.zeros_like(acc_in)

    def weights_fine(row):
        acc_up[...] += dot_lanes(gp4m[pl.ds(row, 3)].reshape(192, half), zj[row + 1])
        acc_in[...] += dot_lanes(gp1m[pl.ds(row, 3)].reshape(192, half), zf[row + 1])

    looped(rows, 4, weights_fine)

    def weights_coarse(index):
        for par in range(2):
            row = 2 * index + par
            acc_mid[...] += dot_lanes(gp3m[par, pl.ds(index, 3)].reshape(96, half), z2[par, index + 1])
            acc_down[...] += dot_lanes(
                gp2m[pl.ds(row, 3)].reshape(96, half),
                zj[pl.ds(2 * row + 1, 2), 128:256, :].reshape(256, half),
            )

    looped(coarse // 2, 4, weights_coarse)

    up = acc_up[...]
    inner = acc_in[...]
    for step in range(3):
        first_up, second_up = up[64 * step : 64 * step + 32], up[64 * step + 32 : 64 * step + 64]
        first_in, second_in = inner[64 * step : 64 * step + 32], inner[64 * step + 32 : 64 * step + 64]
        at = slice(32 * step, 32 * step + 32)
        for part in range(2):
            cols = slice(128 * part, 128 * part + 128)
            grads_out[96 * part + 32 * step : 96 * part + 32 * step + 32, :] = first_up[:, cols] + rolled(
                second_up[:, cols], -32
            )
        grads_out[at, 96:120] = first_in[:, 0:24] + second_in[:, 8:32]
    down = acc_down[...]
    for tap, (step, side) in enumerate(((2, 1), (1, 0), (1, 1), (0, 0))):
        grads_out[192 + 32 * tap : 224 + 32 * tap, :] = down[
            32 * step : 32 * step + 32, 128 * side : 128 * side + 128
        ]
    grads_out[320:416, 0:96] = acc_mid[...]
    k_index = iota((16, 256), 0) % 8
    c_index = iota((16, 256), 1) // 32
    same = (k_index % 4 == c_index // 2) & (k_index // 4 == c_index % 2)
    heads = jnp.where(same, acc_head[...], 0.0)
    for kind in range(2):
        line = jnp.sum(heads[8 * kind : 8 * kind + 8], axis=0, keepdims=True)
        line = line[:, :128] + line[:, 128:]
        line = line + rolled(line, 64)
        line = line + rolled(line, 32)
        grads_out[320 + kind : 321 + kind, 96:128] = line[:, 96:128]


def unpack_kernel(sizes, *refs):
    n_band, own, lon_count = sizes
    low, high = refs[0], refs[1]
    means = refs[2 : 2 + n_band]
    mean_out, grad_in, grad_down, grad_mid, grad_up, grad_head, wide = refs[2 + n_band :]
    me = lax.axis_index("band")
    core = lax.rem(lax.axis_index("group"), 2)
    own_tiles = own // LANES
    first = jnp.where(core == 0, low[...], high[...])
    second = jnp.where(core == 0, high[...], low[...])
    both = jnp.concatenate([first, second], axis=0)
    lane = lax.broadcasted_iota(jnp.int32, (96, LANES), 1)
    part_a, part_b = both[0:96], both[96:192]
    mid = both[320:416]
    for tap_col in range(3):
        ups = jnp.where(lane < 32, rolled(part_a, -32 * tap_col), rolled(part_b, 32 - 32 * tap_col))
        ins = rolled(part_a, -96 - 8 * tap_col)
        mids = rolled(mid, -32 * tap_col)
        for tap_row in range(3):
            at = slice(32 * (2 - tap_row), 32 * (2 - tap_row) + 32)
            grad_up[tap_row, tap_col] = ups[at, 0:64]
            grad_in[tap_row, tap_col] = ins[at, 0:8]
            grad_mid[tap_row, tap_col] = mids[at, 0:32]
    down = both[192:320]
    for tap_col in range(4):
        downs = rolled(down, -32 * tap_col)
        for tap_row in range(4):
            grad_down[tap_row, tap_col] = downs[32 * tap_row : 32 * tap_row + 32, 0:32]
    grad_head[...] = rolled(mid[0:8], -96)[0:2, 0:32]
    for shift in range(n_band):
        origin = lax.rem(me - shift + n_band, n_band)
        for tile in range(own_tiles):
            at = pl.multiple_of((origin * own_tiles + tile) * LANES, LANES)
            wide[:, pl.ds(at, LANES)] = means[shift][tile]
    mean_out[0] = wide[:, 0:lon_count]


def phased(taps):
    before = jnp.pad(taps, ((0, 0), (0, 0), (0, 1), (0, 0)))
    after = jnp.pad(taps, ((0, 0), (0, 0), (1, 0), (0, 0)))
    return jnp.stack([before, after])


def parted(taps, axis):
    first = lax.rev(lax.slice_in_dim(taps, 1, 4, 2, axis), (axis,))
    second = lax.rev(lax.slice_in_dim(taps, 0, 3, 2, axis), (axis,))
    at_end = [(0, 0)] * taps.ndim
    at_start = [(0, 0)] * taps.ndim
    at_end[axis] = (0, 1)
    at_start[axis] = (1, 0)
    return jnp.stack([jnp.pad(first, at_end), jnp.pad(second, at_start)])


def matrices(w_in, w_down, w_mid, w_up, w_head):
    w1 = phased(jnp.transpose(w_in, (2, 0, 1, 3))).reshape(64, 96)
    wd = jnp.transpose(w_down, (2, 0, 1, 3)).reshape(32, 512)
    wm = jnp.transpose(w_mid, (2, 0, 1, 3)).reshape(32, 288)
    up = jnp.transpose(w_up.reshape(3, 3, 32, 2, 32), (2, 0, 3, 1, 4)).reshape(32, 6, 3, 32)
    wu = phased(up).reshape(64, 768)
    sel = np.zeros((8, 8), np.float32)
    for phase in range(2):
        for row in range(4):
            sel[phase * 4 + row, row * 2 + phase] = 1.0
    wh = (jnp.asarray(sel, BF16)[None, :, :, None] * w_head[:, None, None, :]).reshape(16, 256)
    back = phased(jnp.transpose(w_up[::-1, ::-1], (3, 0, 1, 2)))
    wf = jnp.transpose(back.reshape(2, 2, 32, 384), (1, 0, 2, 3)).reshape(128, 384)
    wmf = jnp.transpose(w_mid[::-1, ::-1], (3, 0, 1, 2)).reshape(32, 288)
    taps = jnp.transpose(w_down, (3, 0, 1, 2))
    taps = parted(parted(taps, 1), 3)
    wbd = jnp.transpose(taps, (1, 0, 2, 3, 4, 5)).reshape(128, 288)
    return w1, wd, wm, wu, wh, wh.T, wf, wmf, wbd


def swapped(values, axis, count, bits):
    return lax.ppermute(values, axis, [(i, i ^ bits) for i in range(count)])


def shifted(values, axis, count, shift):
    return lax.ppermute(values, axis, [(i, (i + shift) % count) for i in range(count)])


def reduced(grads, mean_tiles, n_band, n_group):
    group = lax.axis_index("group")
    band = lax.axis_index("band")
    core, chip = group % 2, group // 2
    chips = n_group // 2
    tile_rows = mean_tiles.shape[1]
    half = grads.shape[0] // 2
    mine = lax.dynamic_slice_in_dim(grads, core * half, half, 0)
    theirs = lax.dynamic_slice_in_dim(grads, (1 - core) * half, half, 0)
    total = mine + swapped(theirs, "group", n_group, 1)
    share = half // chips
    kept = lax.dynamic_slice_in_dim(total, chip * share, share, 0)
    got = [
        swapped(lax.dynamic_slice_in_dim(total, (chip ^ k) * share, share, 0), "group", n_group, 2 * k)
        for k in range(1, chips)
    ]
    for piece in got:
        kept = kept + piece
    means = [lax.dynamic_index_in_dim(mean_tiles, band, 0, keepdims=False)]
    arrived = []
    for k in range(1, n_band):
        target = lax.rem(band + k, n_band)
        sent = jnp.concatenate([kept, lax.dynamic_index_in_dim(mean_tiles, target, 0, keepdims=False)])
        arrived.append(shifted(sent, "band", n_band, k))
    for piece in arrived:
        kept = kept + piece[:share]
        means.append(piece[share:])
    pieces = [(chip, kept)] + [
        (chip ^ k, swapped(kept, "group", n_group, 2 * k)) for k in range(1, chips)
    ]
    whole = jnp.zeros((chips, share, LANES), F32)
    for at, piece in pieces:
        whole = lax.dynamic_update_slice(whole, piece[None], (at, 0, 0))
    whole = whole.reshape(half, LANES)
    return whole, swapped(whole, "group", n_group, 1), means


def vmem(*shape, dtype=BF16):
    return pltpu.VMEM(shape, dtype)


def local(
    station_rows,
    station_lons,
    station_obs,
    station_live,
    block_band,
    truth_field,
    length_scales,
    w_in,
    w_down,
    w_mid,
    w_up,
    w_head,
):
    n_band = lax.axis_size("band")
    n_group = lax.axis_size("group")
    n_blocks = station_rows.shape[1]
    lon_count = truth_field.shape[2]
    own_tiles = -(-(-(-lon_count // LANES)) // n_band)
    own = own_tiles * LANES
    window = own + 2 * HALO
    half = window // 2
    rows = ROWS_BAND * n_band
    coarse = rows // 2
    hist_tiles = (window + 2 * REACH) // LANES

    field = truth_field[0]
    total_tiles = n_band * own_tiles + 1
    extended = jnp.concatenate(
        [field[:, lon_count - HALO :], field, field[:, : total_tiles * LANES - HALO - lon_count]], axis=1
    )
    truth_rows = jnp.transpose(extended.reshape(ROWS_BAND, total_tiles, LANES), (1, 0, 2)).reshape(-1, LANES)
    fill = -truth_rows.shape[0] % 8
    band_rows = jnp.zeros((8, LANES), F32).at[0, :n_blocks].set(block_band[0, :, 0].astype(F32))
    pay = jnp.concatenate(
        [
            station_rows[0].astype(F32),
            jnp.where(station_live[0] > 0, station_lons[0].astype(F32), FAR),
            station_obs[0],
            band_rows,
            jnp.pad(truth_rows, ((0, fill), (0, 0))),
        ]
    )
    pays = [pay] + [shifted(pay, "band", n_band, k) for k in range(1, n_band)]
    mats = matrices(w_in, w_down, w_mid, w_up, w_head)

    in_vmem = pl.BlockSpec(memory_space=pltpu.VMEM)
    in_smem = pl.BlockSpec(memory_space=pltpu.SMEM)
    grads, mean_tiles = pl.pallas_call(
        functools.partial(network_kernel, (n_band, n_blocks, own, lon_count)),
        out_shape=(
            jax.ShapeDtypeStruct((416, LANES), F32),
            jax.ShapeDtypeStruct((n_band, own_tiles, ROWS_BAND, LANES), F32),
        ),
        in_specs=[in_vmem] * n_band + [in_smem] + [in_vmem] * len(mats),
        out_specs=(in_vmem, in_vmem),
        scratch_shapes=[
            pltpu.SMEM((n_band, 8, LANES), F32),
            vmem(n_band, hist_tiles * 32, LANES, dtype=F32),
            vmem(4, 4 * LANES, 2 * LANES),
            vmem(rows + 2, 32, half),
            vmem(rows, 64, half, dtype=F32),
            vmem(rows + 2, 256, half),
            vmem(coarse, 32, half, dtype=F32),
            vmem(2, coarse // 2 + 2, 96, half),
            vmem(coarse, 32, half, dtype=F32),
            vmem(rows, 64, half, dtype=F32),
            vmem(rows, 64, half),
            vmem(n_band, 8, half, dtype=F32),
            vmem(n_band, 16, 2 * half),
            vmem(rows + 2, 128, half),
            vmem(rows + 2, 64, half),
            vmem(rows, 64, half),
            vmem(2, coarse // 2 + 2, 32, half),
            vmem(2, coarse // 2 + 2, 96, half),
            vmem(coarse + 2, 32, half),
            vmem(coarse + 2, 96, half),
            vmem(rows + 2, 64, half),
            vmem(n_band, n_blocks, LANES, dtype=F32),
            vmem(n_band, n_blocks, LANES, dtype=F32),
            vmem(192, 256, dtype=F32),
            vmem(96, 256, dtype=F32),
            vmem(96, 96, dtype=F32),
            vmem(192, 32, dtype=F32),
            vmem(16, 256, dtype=F32),
        ],
        compiler_params=pltpu.CompilerParams(vmem_limit_bytes=40 * 1024 * 1024),
    )(*pays, length_scales, *mats)

    low, high, means = reduced(grads, mean_tiles.reshape(n_band, own_tiles * ROWS_BAND, LANES), n_band, n_group)
    means = [piece.reshape(own_tiles, ROWS_BAND, LANES) for piece in means]
    return pl.pallas_call(
        functools.partial(unpack_kernel, (n_band, own, lon_count)),
        out_shape=(
            jax.ShapeDtypeStruct((1, ROWS_BAND, lon_count), F32),
            jax.ShapeDtypeStruct((3, 3, 32, 8), F32),
            jax.ShapeDtypeStruct((4, 4, 32, 32), F32),
            jax.ShapeDtypeStruct((3, 3, 32, 32), F32),
            jax.ShapeDtypeStruct((3, 3, 32, 64), F32),
            jax.ShapeDtypeStruct((2, 32), F32),
        ),
        in_specs=[in_vmem] * (2 + n_band),
        out_specs=(in_vmem,) * 6,
        scratch_shapes=[vmem(ROWS_BAND, n_band * own, dtype=F32)],
        compiler_params=pltpu.CompilerParams(vmem_limit_bytes=16 * 1024 * 1024),
    )(low, high, *means)


def solution(mesh):
    return jax.shard_map(
        local,
        mesh=mesh,
        in_specs=(
            P("group", "band", None),
            P("group", "band", None),
            P("group", "band", None),
            P("group", "band", None),
            P("group", "band", None),
            P("group", "band", None),
            P(),
            P(),
            P(),
            P(),
            P(),
            P(),
        ),
        out_specs=(P("group", "band", None), P(), P(), P(), P(), P()),
        check_vma=False,
    )
```

```python
import functools

import jax
import jax.numpy as jnp
from jax import lax
from jax.experimental import pallas as pl
from jax.experimental.pallas import tpu as pltpu
from jax.sharding import PartitionSpec as P

LANES = 128
HALO = 64
REACH = 128
ROWS_BAND = 4
FAR = -1.0e6
F32 = jnp.float32
BF16 = jnp.bfloat16


def looped(count, step, body):
    step = min(step, count)
    if count == step:
        for index in range(count):
            body(index)
    else:

        def turn(outer, carry):
            for inner in range(step):
                body(outer * step + inner)
            return carry

        lax.fori_loop(0, count // step, turn, 0)


def dot(first, second):
    return jnp.dot(first, second, preferred_element_type=F32)


def dot_lanes(first, second):
    return lax.dot_general(first, second, (((1,), (1,)), ((), ())), preferred_element_type=F32)


def iota(shape, dim):
    return lax.broadcasted_iota(jnp.int32, shape, dim)


def rolled(values, shift):
    width = values.shape[-1]
    return pltpu.roll(values, shift % width, values.ndim - 1)


def four_shifts(even, odd):
    return jnp.concatenate([rolled(odd, 1), even, odd, rolled(even, -1)], axis=0)


def three_shifts(values, width):
    return jnp.concatenate([rolled(values, width), values, rolled(values, -width)], axis=0)


def sigmoid(values):
    return 1.0 / (1.0 + jnp.exp(-values))


def silu(values):
    return values * sigmoid(values)


def silu_slope(values):
    squash = sigmoid(values)
    return squash * (1.0 + values * (1.0 - squash))


def split_three(values):
    high = values.astype(BF16).astype(F32)
    rest = values - high
    middle = rest.astype(BF16).astype(F32)
    return high, middle, rest - middle


def station_sums(own, lon_count, n_blocks, step, me, pay, bands, scales, hist, hi_pos, lo_pos):
    hist_tiles = hist.shape[1] // 32
    start = (me * own - HALO - REACH).astype(F32)
    place = pay[n_blocks : 2 * n_blocks] - start
    place = jnp.where(place < 0.0, place + lon_count, place)
    place = jnp.where(place < 0.0, place + lon_count, place)
    place = jnp.where(place >= lon_count, place - lon_count, place)
    tile_of = jnp.floor(place * (1.0 / LANES))
    hi_pos[...] = tile_of
    lo_pos[...] = place - tile_of * LANES

    m_index = iota((32, 1), 0)
    row_of = (m_index // 8).astype(F32)
    scale_of = (m_index % 8) // 2
    kind_of = m_index % 2
    spread = jnp.where(
        scale_of == 0, scales[0], jnp.where(scale_of == 1, scales[1], jnp.where(scale_of == 2, scales[2], scales[3]))
    )
    rate = -0.5 / (spread * spread)
    lane_iota = iota((LANES, LANES), 0).astype(F32)

    def one_block(block):
        at_row = pay[pl.ds(block, 1), :]
        observed = pay[pl.ds(2 * n_blocks + block, 1), :]
        high = hi_pos[pl.ds(block, 1), :]
        low = lo_pos[pl.ds(block, 1), :]
        gap = row_of - at_row
        left = jnp.exp(gap * gap * rate) * jnp.where(kind_of == 0, 1.0, observed)
        spread_left = jnp.concatenate(
            [jnp.where(high == float(tile), left, 0.0) for tile in range(hist_tiles)], axis=0
        ).astype(BF16)
        one_hot = jnp.where(lane_iota == low, 1.0, 0.0).astype(BF16)
        band = bands[0, block].astype(jnp.int32)
        hist[band] = hist[band] + dot_lanes(spread_left, one_hot)

    looped(n_blocks, step, one_block)


def pack_kernel(sizes, *refs):
    n_band, n_blocks, own, lon_count = sizes
    pays = refs[6 : 6 + n_band]
    wide = refs[6 + n_band]
    held, sems = refs[7 + n_band : 13 + n_band], refs[13 + n_band]
    copies = [pltpu.make_async_copy(refs[k], held[k], sems.at[k]) for k in range(6)]
    for copy in copies:
        copy.start()
    for copy in copies:
        copy.wait()
    rows, lons, obs, live, block_band, field = held
    me = lax.axis_index("band")
    at_row = rows[0].astype(F32)
    lon = jnp.where(live[0] > 0, lons[0].astype(F32), FAR)
    total = wide.shape[1]
    wide[:, 0:HALO] = field[0, :, lon_count - HALO : lon_count]
    wide[:, HALO : HALO + lon_count] = field[0]
    wide[:, HALO + lon_count : total] = field[0, :, 0 : total - HALO - lon_count]
    for shift in range(n_band):
        pay = pays[shift]
        pay[0:n_blocks] = at_row
        pay[n_blocks : 2 * n_blocks] = lon
        pay[2 * n_blocks : 3 * n_blocks] = obs[0]
        pay[3 * n_blocks : 3 * n_blocks + 8] = jnp.zeros((8, LANES), F32)
        pay[3 * n_blocks : 3 * n_blocks + 1, 0:n_blocks] = block_band[...].astype(F32)
        target = lax.rem(me + shift, n_band)
        for tile in range((own + 2 * HALO) // LANES):
            at = pl.multiple_of(target * own + tile * LANES, LANES)
            first = 3 * n_blocks + 8 + ROWS_BAND * tile
            pay[first : first + ROWS_BAND] = wide[:, pl.ds(at, LANES)]


def early_kernel(sizes, *refs):
    n_band, n_blocks, own, lon_count = sizes
    pay, scales, hist, table, token, bands, hi_pos, lo_pos = refs
    me = lax.axis_index("band")
    token[...] = jnp.zeros_like(token)
    pltpu.sync_copy(pay.at[pl.ds(3 * n_blocks, 8)], bands)
    hist[...] = jnp.zeros_like(hist)
    step = n_blocks if n_band <= 4 else 4
    station_sums(own, lon_count, n_blocks, step, me, pay, bands, scales, hist, hi_pos, lo_pos)

    place_in = iota((4 * LANES, 2 * LANES), 0)
    place_out = iota((4 * LANES, 2 * LANES), 1)
    distance = (place_in - (REACH + 2 * (place_out % LANES) + place_out // LANES)).astype(F32)
    squared = distance * distance
    for scale in range(4):
        table[scale] = jnp.exp(squared * (-0.5 / (scales[scale] * scales[scale]))).astype(BF16)


def matrix_kernel(*refs):
    w_in, w_down, w_mid, w_up, w_head, _ = refs[:6]
    w1, wd, wm, wu, wh, wht, wf, wmf, wbd = refs[6:15]
    t1, td, tm, tu, tf, tmf, tbd = refs[15:]
    t1[...] = jnp.zeros_like(t1)
    tu[...] = jnp.zeros_like(tu)
    tf[...] = jnp.zeros_like(tf)
    tbd[...] = jnp.zeros_like(tbd)
    for row in range(3):
        for col in range(3):
            inner = w_in[row, col].astype(F32)
            mid = w_mid[row, col].astype(F32)
            up = w_up[row, col].astype(F32)
            tm[:, (row * 3 + col) * 32 : (row * 3 + col) * 32 + 32] = mid
            back = (2 - row) * 3 + 2 - col
            tmf[back * 32 : back * 32 + 32, 0:32] = mid
            for phase in range(2):
                at = row * 32 + (phase + col) * 8
                t1[at : at + 8, phase * 32 : phase * 32 + 32] = inner
                for part in range(2):
                    cols = slice(part * 32, part * 32 + 32)
                    at = (row * 2 + part) * 128 + (phase + col) * 32
                    tu[phase * 32 : phase * 32 + 32, at : at + 32] = up[:, cols]
                    at = (2 - row) * 128 + (phase + 2 - col) * 32
                    to = part * 64 + phase * 32
                    tf[at : at + 32, to : to + 32] = up[:, cols]
    sides = (((1, 0), (3, -1)), ((0, 1), (2, 0)))
    for row in range(4):
        for col in range(4):
            td[:, (row * 4 + col) * 32 : (row * 4 + col) * 32 + 32] = w_down[row, col].astype(F32)
    for side in range(2):
        for phase in range(2):
            for row, row_shift in sides[side]:
                for col, col_shift in sides[phase]:
                    at = (row_shift + 1) * 96 + (col_shift + 1) * 32
                    to = (side * 2 + phase) * 32
                    tbd[at : at + 32, to : to + 32] = w_down[row, col].astype(F32)
    w1[...] = t1[...].T[0:64, 0:96].astype(BF16)
    wd[...] = td[...].astype(BF16)
    wm[...] = tm[...].astype(BF16)
    wu[...] = tu[...].astype(BF16)
    wf[...] = tf[...].T.astype(BF16)
    wmf[...] = tmf[...].T[0:32, 0:288].astype(BF16)
    wbd[...] = tbd[...].T[:, 0:288].astype(BF16)
    heads = w_head[...].astype(F32)
    heads = jnp.concatenate([heads, jnp.zeros((6, 32), F32)], axis=0)
    heads = jnp.concatenate([heads, jnp.zeros((8, 96), F32)], axis=1)
    heads = heads + rolled(heads, 32)
    heads = heads + rolled(heads, 64)
    heads = jnp.concatenate([heads, heads], axis=1)
    k_index = iota((128, 256), 0)
    c_index = iota((128, 256), 1) // 32
    same = (k_index % 4 == c_index // 2) & ((k_index // 4) % 2 == c_index % 2) & (k_index < 16)
    full = jnp.where(same, jnp.where(k_index < 8, heads[0:1], heads[1:2]), 0.0)
    wh[...] = full[0:16].astype(BF16)
    wht[...] = full.T[:, 0:16].astype(BF16)


def network_kernel(sizes, *refs):
    n_band, n_blocks, own, lon_count = sizes
    window = own + 2 * HALO
    half = window // 2
    rows = ROWS_BAND * n_band
    coarse = rows // 2
    own_tiles = own // LANES
    pays = refs[:n_band]
    (scales, hist_own, table, w1, wd, wm, wu, wh, wht, wf, wmf, wbd) = refs[n_band : n_band + 12]
    hist, grads_out, mean_out = refs[n_band + 12 : n_band + 15]
    (
        bands, band_sems, zf, p1, zj, p2, z2, p3, p4, h4, truth, mean_split,
        gs, gp4m, gj, gp3m, zg3, gp2m, zg2, gp1m, hi_pos, lo_pos,
        acc_up, acc_down, acc_mid, acc_in, acc_head,
    ) = refs[n_band + 15 :]
    many = n_band > 4
    me = lax.axis_index("band")
    cell_count = float(rows * lon_count)

    copies = [
        pltpu.make_async_copy(pays[k].at[pl.ds(3 * n_blocks, 8)], bands.at[k], band_sems.at[k])
        for k in range(1, n_band)
    ]
    for copy in copies:
        copy.start()
    for copy in copies:
        copy.wait()
    for source in range(1, n_band):
        station_sums(
            own, lon_count, n_blocks, 4 if many else n_blocks, me, pays[source], bands.at[source], scales,
            hist, hi_pos.at[source], lo_pos.at[source],
        )

    all_rows = 32 * n_band
    channel = iota((all_rows, 1), 0) % 8
    feats = []
    for chunk in range(half // LANES):
        tiles = [
            hist[:, (2 * chunk + t) * 32 : (2 * chunk + t + 1) * 32, :].reshape(all_rows, LANES)
            for t in range(4)
        ]
        cells = jnp.concatenate(tiles, axis=1)
        high = cells.astype(BF16)
        low = (cells - high.astype(F32)).astype(BF16)
        total = None
        for scale in range(4):
            keep = (channel // 2 == scale).astype(F32).astype(BF16)
            part = dot(high * keep, table[scale]) + dot(low * keep, table[scale])
            total = part if total is None else total + part
        below = pltpu.roll(total, 1, 0)
        density = jnp.where(channel % 2 == 0, total, below)
        feats.append(total / (1.0 + density))
    even = jnp.concatenate([f[:, :LANES] for f in feats], axis=1)
    odd = jnp.concatenate([f[:, LANES:] for f in feats], axis=1)
    odd_before = rolled(odd, 1)
    even_after = rolled(even, -1)
    for edge in (0, rows + 1):
        zf[edge] = jnp.zeros((32, half), BF16)
        zj[edge] = jnp.zeros((256, half), BF16)
        gs[edge] = jnp.zeros((128, half), BF16)
        gp4m[edge] = jnp.zeros((64, half), BF16)
        gp1m[edge] = jnp.zeros((64, half), BF16)
    for edge in (0, coarse + 1):
        zg2[edge] = jnp.zeros((96, half), BF16)
        gp2m[edge] = jnp.zeros((32, half), BF16)
    for edge in (0, coarse // 2 + 1):
        for par in range(2):
            z2[par, edge] = jnp.zeros((96, half), BF16)
            zg3[par, edge] = jnp.zeros((96, half), BF16)
            gp3m[par, edge] = jnp.zeros((32, half), BF16)
    for row in range(rows):
        pick = slice(row * 8, row * 8 + 8)
        zf[row + 1] = jnp.concatenate(
            [odd_before[pick], even[pick], odd[pick], even_after[pick]], axis=0
        ).astype(BF16)

    fine_iota = iota((2 * LANES, 2 * LANES), 0)
    part_iota = iota((2 * LANES, 2 * LANES), 1)
    parting = (fine_iota == 2 * (part_iota % LANES) + part_iota // LANES).astype(F32).astype(BF16)
    chunks = window // (2 * LANES)
    for source in range(n_band):
        at = lax.rem(me - source + n_band, n_band)
        pieces = []
        for chunk in range(2):
            if chunk < chunks:
                tiles = [
                    pays[source][
                        3 * n_blocks + 8 + (2 * chunk + t) * ROWS_BAND : 3 * n_blocks + 8 + (2 * chunk + t + 1) * ROWS_BAND
                    ]
                    for t in range(2)
                ]
                pieces.append(jnp.concatenate(tiles, axis=1))
            else:
                pieces.append(jnp.zeros((ROWS_BAND, 2 * LANES), F32))
        stacked = jnp.concatenate(split_three(jnp.concatenate(pieces, axis=0)) + (jnp.zeros((8, 2 * LANES), F32),), axis=0)
        parted = dot(stacked.astype(BF16), parting)
        parted = parted[0:8] + parted[8:16] + parted[16:24]
        for chunk in range(chunks):
            for phase in range(2):
                truth[at, phase * 4 : phase * 4 + 4, chunk * LANES : (chunk + 1) * LANES] = parted[
                    chunk * 4 : chunk * 4 + 4, phase * LANES : (phase + 1) * LANES
                ]

    def first(row):
        pre = dot(w1[...], zf[pl.ds(row, 3)].reshape(96, half))
        p1[row] = pre
        hidden = silu(pre)
        zj[row + 1, 128:256, :] = four_shifts(hidden[:32], hidden[32:]).astype(BF16)

    looped(rows, 4 if many else rows, first)

    def second(index):
        for par in range(2):
            row = 2 * index + par
            pre = dot(wd[...], zj[pl.ds(2 * row, 4), 128:256, :].reshape(512, half))
            p2[row] = pre
            z2[par, index + 1] = three_shifts(silu(pre), 2).astype(BF16)

    looped(coarse // 2, 4 if many else coarse // 2, second)

    def third(index):
        for par in range(2):
            row = 2 * index + par
            pre = dot(wm[...], z2[par, pl.ds(index, 3)].reshape(288, half))
            p3[row] = pre
            hidden = silu(pre)
            wide = four_shifts(hidden, hidden).astype(BF16)
            zj[2 * row + 1, 0:128, :] = wide
            zj[2 * row + 2, 0:128, :] = wide

    looped(coarse // 2, 4 if many else coarse // 2, third)

    def fourth(row):
        pre = dot(wu[...], zj[pl.ds(row, 3)].reshape(768, half))
        p4[row] = pre
        h4[row] = silu(pre).astype(BF16)

    looped(rows, 4 if many else rows, fourth)

    own_cells = jnp.clip(lon_count - me * own, 0, own) // 2
    place = iota((1, half), 1)
    mask = ((place >= HALO // 2) & (place < HALO // 2 + own_cells)).astype(F32)
    acc_head[...] = jnp.zeros_like(acc_head)

    def head(group):
        hidden = h4[pl.ds(4 * group, 4)].reshape(256, half)
        out = dot(wh[...], hidden)
        mean = out[:8]
        raw = out[8:]
        decay = jnp.exp(-jnp.abs(raw))
        noise = 0.1 + (jnp.maximum(raw, 0.0) + jnp.log1p(decay))
        error = (mean - truth[group]) / noise
        weight = 1.0 / (noise * cell_count)
        grad_mean = error * weight
        grad_raw = (1.0 - error * error) * weight * sigmoid(raw)
        grad_out = jnp.concatenate([grad_mean, grad_raw], axis=0)
        grad_bf = grad_out.astype(BF16)
        acc_head[...] += dot_lanes((grad_out * mask).astype(BF16), hidden)
        back = dot(wht[...], grad_bf)
        pre = p4[pl.ds(4 * group, 4)].reshape(256, half)
        grad = back * silu_slope(pre)
        for row in range(4):
            mine = grad[row * 64 : row * 64 + 64]
            gp4m[4 * group + row + 1] = (mine * mask).astype(BF16)
            gs[4 * group + row + 1] = four_shifts(mine[:32], mine[32:]).astype(BF16)
        parts = split_three(jnp.concatenate([mean[0:4], mean[4:8]], axis=1))
        mean_split[group] = jnp.concatenate(
            parts + (jnp.zeros((4, 2 * half), F32),), axis=0
        ).astype(BF16)

    looped(n_band, 1 if many else n_band, head)

    target = iota((2 * half, own), 1) + HALO
    origin = iota((2 * half, own), 0)
    joining = (target == 2 * (origin % half) + origin // half).astype(F32).astype(BF16)
    joined = dot(mean_split[...].reshape(16 * n_band, 2 * half), joining)
    for band in range(n_band):
        four = joined[16 * band : 16 * band + 8] + joined[16 * band + 8 : 16 * band + 16]
        four = four[0:4] + four[4:8]
        for tile in range(own_tiles):
            mean_out[band, tile] = four[:, tile * LANES : (tile + 1) * LANES]

    def join_back(index):
        for par in range(2):
            row = 2 * index + par
            total = None
            for side in range(2):
                fine = 2 * row + side
                back = dot(wf[...], gs[pl.ds(fine, 3)].reshape(384, half)).astype(BF16)
                gj[fine] = back[64:]
                up = back[:64].astype(F32)
                part = up[:32] + up[32:]
                total = part if total is None else total + part
            grad = total * silu_slope(p3[row])
            gp3m[par, index + 1] = (grad * mask).astype(BF16)
            zg3[par, index + 1] = three_shifts(grad, 2).astype(BF16)

    looped(coarse // 2, 2 if many else coarse // 2, join_back)

    def mid_back(index):
        for par in range(2):
            row = 2 * index + par
            back = dot(wmf[...], zg3[par, pl.ds(index, 3)].reshape(288, half))
            grad = back * silu_slope(p2[row])
            gp2m[row + 1] = (grad * mask).astype(BF16)
            zg2[row + 1] = three_shifts(grad, 1).astype(BF16)

    looped(coarse // 2, 4 if many else coarse // 2, mid_back)

    def down_back(row):
        back = dot(wbd[...], zg2[pl.ds(row, 3)].reshape(288, half))
        for side in range(2):
            fine = 2 * row + side
            grad = (back[64 * side : 64 * side + 64] + gj[fine].astype(F32)) * silu_slope(p1[fine])
            gp1m[fine + 1] = (grad * mask).astype(BF16)

    looped(coarse, 4 if many else coarse, down_back)

    acc_up[...] = jnp.zeros_like(acc_up)
    acc_down[...] = jnp.zeros_like(acc_down)
    acc_mid[...] = jnp.zeros_like(acc_mid)
    acc_in[...] = jnp.zeros_like(acc_in)

    def weights_fine(row):
        acc_up[...] += dot_lanes(gp4m[pl.ds(row, 3)].reshape(192, half), zj[row + 1])
        acc_in[...] += dot_lanes(zf[row + 1], gp1m[pl.ds(row, 3)].reshape(192, half))

    looped(rows, 4 if many else rows, weights_fine)

    def weights_coarse(index):
        for par in range(2):
            row = 2 * index + par
            acc_mid[...] += dot_lanes(gp3m[par, pl.ds(index, 3)].reshape(96, half), z2[par, index + 1])
            acc_down[...] += dot_lanes(
                gp2m[pl.ds(row, 3)].reshape(96, half),
                zj[pl.ds(2 * row + 1, 2), 128:256, :].reshape(256, half),
            )

    looped(coarse // 2, 4 if many else coarse // 2, weights_coarse)

    up = acc_up[...]
    for step in range(3):
        first_up, second_up = up[64 * step : 64 * step + 32], up[64 * step + 32 : 64 * step + 64]
        for part in range(2):
            cols = slice(128 * part, 128 * part + 128)
            grads_out[96 * part + 32 * step : 96 * part + 32 * step + 32, :] = first_up[:, cols] + rolled(
                second_up[:, cols], -32
            )
    mid = acc_mid[...]
    grads_out[0:96, 96:128] = mid[:, 0:32]
    grads_out[96:192, 96:128] = mid[:, 32:64]
    down = acc_down[...]
    for tap, (step, side) in enumerate(((2, 1), (1, 0), (1, 1), (0, 0))):
        grads_out[192 + 32 * tap : 224 + 32 * tap, :] = down[
            32 * step : 32 * step + 32, 128 * side : 128 * side + 128
        ]
    inner = acc_in[...]
    for step in range(3):
        grads_out[320:344, 32 * step : 32 * step + 32] = (
            inner[0:24, 64 * step : 64 * step + 32] + inner[8:32, 64 * step + 32 : 64 * step + 64]
        )
    for part in range(4):
        grads_out[344:368, 32 * part : 32 * part + 32] = mid[24 * part : 24 * part + 24, 64:96]
    grads_out[320:344, 96:128] = jnp.zeros((24, 32), F32)
    grads_out[368:384] = jnp.zeros((16, LANES), F32)
    k_index = iota((16, 256), 0) % 8
    c_index = iota((16, 256), 1) // 32
    same = (k_index % 4 == c_index // 2) & (k_index // 4 == c_index % 2)
    heads = jnp.where(same, acc_head[...], 0.0)
    for kind in range(2):
        line = jnp.sum(heads[8 * kind : 8 * kind + 8], axis=0, keepdims=True)
        line = line[:, :128] + line[:, 128:]
        line = line + rolled(line, 64)
        line = line + rolled(line, 32)
        grads_out[320 + kind : 321 + kind, 96:128] = line[:, 96:128]


def unpack_kernel(sizes, *refs):
    n_band, own, lon_count = sizes
    low, high = refs[0], refs[1]
    means = refs[2 : 2 + n_band]
    mean_out, grad_in, grad_down, grad_mid, grad_up, grad_head, wide = refs[2 + n_band :]
    me = lax.axis_index("band")
    core = lax.rem(lax.axis_index("group"), 2)
    own_tiles = own // LANES
    first = jnp.where(core == 0, low[...], high[...])
    second = jnp.where(core == 0, high[...], low[...])
    part_a, part_b = first[0:96], first[96:192]
    down, inner, folded = second[0:128], second[128:152], second[152:176]
    last = jnp.concatenate([rolled(folded, -32 * part) for part in range(4)], axis=0)
    lane = iota((96, LANES), 1)
    mids = (rolled(part_a, -96), rolled(part_b, -96), last)
    for tap_col in range(3):
        ups = jnp.where(lane < 32, rolled(part_a, -32 * tap_col), rolled(part_b, 32 - 32 * tap_col))
        for tap_row in range(3):
            at = slice(32 * (2 - tap_row), 32 * (2 - tap_row) + 32)
            grad_up[tap_row, tap_col] = ups[at, 0:64]
            grad_mid[tap_row, tap_col] = mids[tap_col][at, 0:32]
    for tap_row in range(3):
        ins = rolled(inner, -32 * (2 - tap_row))
        for tap_col in range(3):
            grad_in[tap_row, tap_col] = ins[8 * tap_col : 8 * tap_col + 8, 0:32]
    for tap_col in range(4):
        downs = rolled(down, -32 * tap_col)
        for tap_row in range(4):
            grad_down[tap_row, tap_col] = downs[32 * tap_row : 32 * tap_row + 32, 0:32]
    grad_head[...] = rolled(inner[0:8], -96)[0:2, 0:32]
    for shift in range(n_band):
        origin = lax.rem(me - shift + n_band, n_band)
        for tile in range(own_tiles):
            at = pl.multiple_of((origin * own_tiles + tile) * LANES, LANES)
            wide[:, pl.ds(at, LANES)] = means[shift][tile]
    mean_out[0] = wide[:, 0:lon_count]


def swapped(values, axis, count, bits):
    return lax.ppermute(values, axis, [(i, i ^ bits) for i in range(count)])


def shifted(values, axis, count, shift):
    return lax.ppermute(values, axis, [(i, (i + shift) % count) for i in range(count)])


def reduced(grads, mean_tiles, n_band, n_group):
    group = lax.axis_index("group")
    band = lax.axis_index("band")
    core, side = group % 2, (group // 2) % 2
    half = grads.shape[0] // 2
    mine = lax.dynamic_slice_in_dim(grads, core * half, half, 0)
    theirs = lax.dynamic_slice_in_dim(grads, (1 - core) * half, half, 0)
    total = mine + swapped(theirs, "group", n_group, 1)
    share = half // 2
    kept = lax.dynamic_slice_in_dim(total, side * share, share, 0)
    other = lax.dynamic_slice_in_dim(total, (1 - side) * share, share, 0)
    got = [swapped(other if k % 2 else kept, "group", n_group, 2 * k) for k in range(1, n_group // 2)]
    for piece in got:
        kept = kept + piece
    means = [lax.dynamic_index_in_dim(mean_tiles, band, 0, keepdims=False)]
    arrived = []
    for k in range(1, n_band):
        target = lax.rem(band + k, n_band)
        sent = jnp.concatenate([kept, lax.dynamic_index_in_dim(mean_tiles, target, 0, keepdims=False)])
        arrived.append(shifted(sent, "band", n_band, k))
    for piece in arrived:
        kept = kept + piece[:share]
        means.append(piece[share:])
    other = swapped(kept, "group", n_group, 2)
    whole = jnp.where(side == 0, jnp.concatenate([kept, other]), jnp.concatenate([other, kept]))
    return whole, swapped(whole, "group", n_group, 1), means


def vmem(*shape, dtype=BF16):
    return pltpu.VMEM(shape, dtype)


def local(
    station_rows,
    station_lons,
    station_obs,
    station_live,
    block_band,
    truth_field,
    length_scales,
    w_in,
    w_down,
    w_mid,
    w_up,
    w_head,
):
    n_band = lax.axis_size("band")
    n_group = lax.axis_size("group")
    n_blocks = station_rows.shape[1]
    lon_count = truth_field.shape[2]
    own_tiles = -(-(-(-lon_count // LANES)) // n_band)
    own = own_tiles * LANES
    window = own + 2 * HALO
    half = window // 2
    rows = ROWS_BAND * n_band
    coarse = rows // 2
    hist_tiles = (window + 2 * REACH) // LANES

    sizes = (n_band, n_blocks, own, lon_count)
    pay_rows = 3 * n_blocks + 8 + -(-(window // LANES) * ROWS_BAND // 8) * 8
    wide_lanes = (n_band * own_tiles + 1) * LANES
    in_vmem = pl.BlockSpec(memory_space=pltpu.VMEM)
    in_smem = pl.BlockSpec(memory_space=pltpu.SMEM)
    in_hbm = pl.BlockSpec(memory_space=pltpu.HBM)

    def shaped(*shape, dtype=BF16):
        return jax.ShapeDtypeStruct(shape, dtype)

    arrays = (
        station_rows, station_lons, station_obs, station_live, block_band.reshape(1, n_blocks), truth_field
    )
    packed = pl.pallas_call(
        functools.partial(pack_kernel, sizes),
        out_shape=(shaped(pay_rows, LANES, dtype=F32),) * n_band,
        in_specs=[in_hbm] * 6,
        out_specs=(in_vmem,) * n_band,
        scratch_shapes=[vmem(ROWS_BAND, wide_lanes, dtype=F32)]
        + [vmem(*arg.shape, dtype=arg.dtype) for arg in arrays]
        + [pltpu.SemaphoreType.DMA((6,))],
        compiler_params=pltpu.CompilerParams(vmem_limit_bytes=56 * 1024 * 1024),
    )(*arrays)
    pays = [packed[0]] + [shifted(packed[k], "band", n_band, k) for k in range(1, n_band)]

    hist_shape = (n_band, hist_tiles * 32, LANES)
    hist, table, token = pl.pallas_call(
        functools.partial(early_kernel, sizes),
        out_shape=(
            shaped(*hist_shape, dtype=F32),
            shaped(4, 4 * LANES, 2 * LANES),
            shaped(8, LANES, dtype=F32),
        ),
        in_specs=[in_vmem, in_smem],
        out_specs=(in_vmem,) * 3,
        scratch_shapes=[
            pltpu.SMEM((8, LANES), F32),
            vmem(n_blocks, LANES, dtype=F32),
            vmem(n_blocks, LANES, dtype=F32),
        ],
        compiler_params=pltpu.CompilerParams(vmem_limit_bytes=16 * 1024 * 1024),
        cost_estimate=pl.CostEstimate(flops=200_000_000, bytes_accessed=2_000_000, transcendentals=700_000),
    )(packed[0], length_scales)
    mats = pl.pallas_call(
        matrix_kernel,
        out_shape=(
            shaped(64, 96),
            shaped(32, 512),
            shaped(32, 288),
            shaped(64, 768),
            shaped(16, 256),
            shaped(256, 16),
            shaped(128, 384),
            shaped(32, 288),
            shaped(128, 288),
        ),
        in_specs=[in_vmem] * 6,
        out_specs=(in_vmem,) * 9,
        scratch_shapes=[
            vmem(128, 128, dtype=F32),
            vmem(32, 512, dtype=F32),
            vmem(32, 288, dtype=F32),
            vmem(64, 768, dtype=F32),
            vmem(384, 128, dtype=F32),
            vmem(384, 128, dtype=F32),
            vmem(384, 128, dtype=F32),
        ],
        compiler_params=pltpu.CompilerParams(vmem_limit_bytes=16 * 1024 * 1024),
        cost_estimate=pl.CostEstimate(flops=10_000_000, bytes_accessed=1_000_000, transcendentals=0),
    )(jnp.transpose(w_in, (0, 1, 3, 2)), w_down, w_mid, w_up, w_head, token)
    early = (hist, table) + tuple(mats)

    _, grads, mean_tiles = pl.pallas_call(
        functools.partial(network_kernel, sizes),
        out_shape=(
            shaped(*hist_shape, dtype=F32),
            shaped(384, LANES, dtype=F32),
            shaped(n_band, own_tiles, ROWS_BAND, LANES, dtype=F32),
        ),
        in_specs=[in_vmem] * n_band + [in_smem] + [in_vmem] * 11,
        out_specs=(in_vmem, in_vmem, in_vmem),
        input_output_aliases={n_band + 1: 0},
        scratch_shapes=[
            pltpu.SMEM((n_band, 8, LANES), F32),
            pltpu.SemaphoreType.DMA((n_band,)),
            vmem(rows + 2, 32, half),
            vmem(rows, 64, half, dtype=F32),
            vmem(rows + 2, 256, half),
            vmem(coarse, 32, half, dtype=F32),
            vmem(2, coarse // 2 + 2, 96, half),
            vmem(coarse, 32, half, dtype=F32),
            vmem(rows, 64, half, dtype=F32),
            vmem(rows, 64, half),
            vmem(n_band, 8, half, dtype=F32),
            vmem(n_band, 16, 2 * half),
            vmem(rows + 2, 128, half),
            vmem(rows + 2, 64, half),
            vmem(rows, 64, half),
            vmem(2, coarse // 2 + 2, 32, half),
            vmem(2, coarse // 2 + 2, 96, half),
            vmem(coarse + 2, 32, half),
            vmem(coarse + 2, 96, half),
            vmem(rows + 2, 64, half),
            vmem(n_band, n_blocks, LANES, dtype=F32),
            vmem(n_band, n_blocks, LANES, dtype=F32),
            vmem(192, 256, dtype=F32),
            vmem(96, 256, dtype=F32),
            vmem(96, 96, dtype=F32),
            vmem(32, 192, dtype=F32),
            vmem(16, 256, dtype=F32),
        ],
        compiler_params=pltpu.CompilerParams(vmem_limit_bytes=40 * 1024 * 1024),
        cost_estimate=pl.CostEstimate(flops=4_000_000_000, bytes_accessed=4_000_000, transcendentals=2_000_000),
    )(*pays, length_scales, *early)

    low, high, means = reduced(grads, mean_tiles.reshape(n_band, own_tiles * ROWS_BAND, LANES), n_band, n_group)
    means = [piece.reshape(own_tiles, ROWS_BAND, LANES) for piece in means]
    outs = pl.pallas_call(
        functools.partial(unpack_kernel, (n_band, own, lon_count)),
        out_shape=(
            jax.ShapeDtypeStruct((1, ROWS_BAND, lon_count), F32),
            jax.ShapeDtypeStruct((3, 3, 8, 32), F32),
            jax.ShapeDtypeStruct((4, 4, 32, 32), F32),
            jax.ShapeDtypeStruct((3, 3, 32, 32), F32),
            jax.ShapeDtypeStruct((3, 3, 32, 64), F32),
            jax.ShapeDtypeStruct((2, 32), F32),
        ),
        in_specs=[in_vmem] * (2 + n_band),
        out_specs=(in_vmem,) * 6,
        scratch_shapes=[vmem(ROWS_BAND, n_band * own, dtype=F32)],
        compiler_params=pltpu.CompilerParams(vmem_limit_bytes=16 * 1024 * 1024),
    )(low, high, *means)
    return (outs[0], jnp.transpose(outs[1], (0, 1, 3, 2))) + tuple(outs[2:])


def solution(mesh):
    return jax.shard_map(
        local,
        mesh=mesh,
        in_specs=(
            P("group", "band", None),
            P("group", "band", None),
            P("group", "band", None),
            P("group", "band", None),
            P("group", "band", None),
            P("group", "band", None),
            P(),
            P(),
            P(),
            P(),
            P(),
            P(),
        ),
        out_specs=(P("group", "band", None), P(), P(), P(), P(), P()),
        check_vma=False,
    )
```

```python
import functools

import jax
import jax.numpy as jnp
from jax import lax
from jax.experimental import pallas as pl
from jax.experimental.pallas import tpu as pltpu
from jax.sharding import PartitionSpec as P

LANES = 128
HALO = 64
REACH = 128
ROWS_BAND = 4
FAR = -1.0e6
F32 = jnp.float32
BF16 = jnp.bfloat16


def looped(count, step, body):
    step = min(step, count)
    if count == step:
        for index in range(count):
            body(index)
    else:

        def turn(outer, carry):
            for inner in range(step):
                body(outer * step + inner)
            return carry

        lax.fori_loop(0, count // step, turn, 0)


def dot(first, second):
    return jnp.dot(first, second, preferred_element_type=F32)


def dot_lanes(first, second):
    return lax.dot_general(first, second, (((1,), (1,)), ((), ())), preferred_element_type=F32)


def iota(shape, dim):
    return lax.broadcasted_iota(jnp.int32, shape, dim)


def rolled(values, shift):
    width = values.shape[-1]
    return pltpu.roll(values, shift % width, values.ndim - 1)


def four_shifts(even, odd):
    return jnp.concatenate([rolled(odd, 1), even, odd, rolled(even, -1)], axis=0)


def three_shifts(values, width):
    return jnp.concatenate([rolled(values, width), values, rolled(values, -width)], axis=0)


def sigmoid(values):
    return 0.5 + 0.5 * jnp.tanh(0.5 * values)


def silu_and_slope(values):
    squash = sigmoid(values)
    hidden = values * squash
    return hidden, squash + hidden * (1.0 - squash)


def split_three(values):
    high = values.astype(BF16).astype(F32)
    rest = values - high
    middle = rest.astype(BF16).astype(F32)
    return high, middle, rest - middle


def station_sums(own, lon_count, n_blocks, step, me, pay, bands, scales, hist, hi_pos, lo_pos):
    hist_tiles = hist.shape[1] // 32
    start = (me * own - HALO - REACH).astype(F32)
    place = pay[n_blocks : 2 * n_blocks] - start
    place = jnp.where(place < 0.0, place + lon_count, place)
    place = jnp.where(place < 0.0, place + lon_count, place)
    place = jnp.where(place >= lon_count, place - lon_count, place)
    tile_of = jnp.floor(place * (1.0 / LANES))
    hi_pos[...] = tile_of
    lo_pos[...] = place - tile_of * LANES

    m_index = iota((32, 1), 0)
    row_of = ((m_index % 8) // 2).astype(F32)
    scale_of = m_index // 8
    kind_of = m_index % 2
    spread = jnp.where(
        scale_of == 0, scales[0], jnp.where(scale_of == 1, scales[1], jnp.where(scale_of == 2, scales[2], scales[3]))
    )
    rate = -0.5 / (spread * spread)
    lane_iota = iota((LANES, LANES), 0).astype(F32)

    def one_block(block):
        at_row = pay[pl.ds(block, 1), :]
        observed = pay[pl.ds(2 * n_blocks + block, 1), :]
        high = hi_pos[pl.ds(block, 1), :]
        low = lo_pos[pl.ds(block, 1), :]
        gap = row_of - at_row
        left = jnp.exp(gap * gap * rate) * jnp.where(kind_of == 0, 1.0, observed)
        spread_left = jnp.concatenate(
            [jnp.where(high == float(tile), left, 0.0) for tile in range(hist_tiles)], axis=0
        ).astype(BF16)
        one_hot = jnp.where(lane_iota == low, 1.0, 0.0).astype(BF16)
        band = bands[0, block].astype(jnp.int32)
        hist[band] = hist[band] + dot_lanes(spread_left, one_hot)

    looped(n_blocks, step, one_block)


def pack_kernel(sizes, *refs):
    n_band, n_blocks, own, lon_count = sizes
    pays = refs[7 : 7 + n_band]
    wide = refs[7 + n_band]
    held, sems = refs[8 + n_band : 15 + n_band], refs[15 + n_band]
    copies = [pltpu.make_async_copy(refs[k], held[k], sems.at[k]) for k in range(7)]
    for copy in copies:
        copy.start()
    for copy in copies:
        copy.wait()
    rows, lons, obs, live, block_band, field, scales = held
    me = lax.axis_index("band")
    at_row = rows[0].astype(F32)
    lon = jnp.where(live[0] > 0, lons[0].astype(F32), FAR)
    total = wide.shape[1]
    wide[:, 0:HALO] = field[0, :, lon_count - HALO : lon_count]
    wide[:, HALO : HALO + lon_count] = field[0]
    wide[:, HALO + lon_count : total] = field[0, :, 0 : total - HALO - lon_count]
    for shift in range(n_band):
        pay = pays[shift]
        pay[0:n_blocks] = at_row
        pay[n_blocks : 2 * n_blocks] = lon
        pay[2 * n_blocks : 3 * n_blocks] = obs[0]
        pay[3 * n_blocks : 3 * n_blocks + 8] = jnp.zeros((8, LANES), F32)
        pay[3 * n_blocks : 3 * n_blocks + 1, 0:n_blocks] = block_band[...].astype(F32)
        pay[3 * n_blocks + 1 : 3 * n_blocks + 2, 0:4] = scales[...]
        target = me ^ shift
        for tile in range((own + 2 * HALO) // LANES):
            at = pl.multiple_of(target * own + tile * LANES, LANES)
            first = 3 * n_blocks + 8 + ROWS_BAND * tile
            pay[first : first + ROWS_BAND] = wide[:, pl.ds(at, LANES)]


def early_kernel(sizes, *refs):
    n_band, n_blocks, own, lon_count = sizes
    pay = refs[0]
    hist, table, w1, wd, wm, wu, wh, wht, wf, wmf, wbd = refs[6:17]
    bands, hi_pos, lo_pos, t1, td, tm, tu, tf, tmf, tbd = refs[17:27]
    held, sems = refs[27:32], refs[32]
    me = lax.axis_index("band")
    band_copy = pltpu.make_async_copy(pay.at[pl.ds(3 * n_blocks, 8)], bands, sems.at[5])
    band_copy.start()
    copies = [pltpu.make_async_copy(refs[1 + k], held[k], sems.at[k]) for k in range(5)]
    for copy in copies:
        copy.start()
    place_in = iota((4 * LANES, 2 * LANES), 0)
    place_out = iota((4 * LANES, 2 * LANES), 1)
    distance = (place_in - (REACH + 2 * (place_out % LANES) + place_out // LANES)).astype(F32)
    squared = distance * distance
    band_copy.wait()
    scales = [bands[1, k] for k in range(4)]
    hist[...] = jnp.zeros_like(hist)
    step = n_blocks if n_band <= 4 else 4
    station_sums(own, lon_count, n_blocks, step, me, pay, bands, scales, hist, hi_pos, lo_pos)
    for scale in range(4):
        table[scale] = jnp.exp(squared * (-0.5 / (scales[scale] * scales[scale]))).astype(BF16)

    for copy in copies:
        copy.wait()
    w_in, w_down, w_mid, w_up, w_head = held
    for held in (t1, tm, tu, tf, tmf, tbd):
        held[...] = jnp.zeros_like(held)
    for row in range(3):
        for col in range(3):
            inner = w_in[row, col].astype(F32)
            mid = w_mid[row, col].astype(F32)
            up = w_up[row, col].astype(F32)
            back = (2 - row) * 3 + 2 - col
            for out in range(4):
                at = out * 96 + (row * 3 + col) * 32
                tm[out * 32 : out * 32 + 32, at : at + 32] = mid
                at = out * 96 + back * 32
                tmf[at : at + 32, out * 32 : out * 32 + 32] = mid
            for phase in range(2):
                for out in range(4):
                    at = (out + row) * 32 + (phase + col) * 8
                    to = out * 64 + phase * 32
                    t1[at : at + 8, to : to + 32] = inner
                for part in range(2):
                    cols = slice(part * 32, part * 32 + 32)
                    at = (row * 2 + part) * 128 + (phase + col) * 32
                    tu[phase * 32 : phase * 32 + 32, at : at + 32] = up[:, cols]
                    at = (2 - row) * 128 + (phase + 2 - col) * 32
                    to = part * 64 + phase * 32
                    tf[at : at + 32, to : to + 32] = up[:, cols]
    sides = (((1, 0), (3, -1)), ((0, 1), (2, 0)))
    for row in range(4):
        for col in range(4):
            td[:, (row * 4 + col) * 32 : (row * 4 + col) * 32 + 32] = w_down[row, col].astype(F32)
    for side in range(2):
        for phase in range(2):
            for row, row_shift in sides[side]:
                for col, col_shift in sides[phase]:
                    for out in range(2):
                        at = (out + row_shift + 1) * 96 + (col_shift + 1) * 32
                        to = out * 128 + (side * 2 + phase) * 32
                        tbd[at : at + 32, to : to + 32] = w_down[row, col].astype(F32)

    def two_rows(one, shift):
        empty = jnp.zeros((one.shape[0], shift), F32)
        return jnp.concatenate(
            [jnp.concatenate([one, empty], axis=1), jnp.concatenate([empty, one], axis=1)], axis=0
        ).astype(BF16)

    w1[...] = t1[...].T[:, 0:192].astype(BF16)
    wd[...] = two_rows(td[...], 256)
    wm[...] = tm[...].astype(BF16)
    wu[...] = two_rows(tu[...], 256)
    wf[...] = two_rows(tf[...].T, 128)
    wmf[...] = tmf[...].T[:, 0:576].astype(BF16)
    wbd[...] = tbd[...].T.astype(BF16)
    heads = w_head[...].astype(F32)
    heads = jnp.concatenate([heads, jnp.zeros((6, 32), F32)], axis=0)
    heads = jnp.concatenate([heads, jnp.zeros((8, 96), F32)], axis=1)
    heads = heads + rolled(heads, 32)
    heads = heads + rolled(heads, 64)
    heads = jnp.concatenate([heads, heads], axis=1)
    k_index = iota((128, 256), 0)
    c_index = iota((128, 256), 1) // 32
    same = (k_index % 4 == c_index // 2) & ((k_index // 4) % 2 == c_index % 2) & (k_index < 16)
    full = jnp.where(same, jnp.where(k_index < 8, heads[0:1], heads[1:2]), 0.0)
    wh[...] = full[0:16].astype(BF16)
    wht[...] = full.T[:, 0:16].astype(BF16)


def network_kernel(sizes, *refs):
    n_band, n_blocks, own, lon_count = sizes
    window = own + 2 * HALO
    half = window // 2
    rows = ROWS_BAND * n_band
    coarse = rows // 2
    own_tiles = own // LANES
    pays = refs[:n_band]
    (hist_own, table, w1, wd, wm, wu, wh, wht, wf, wmf, wbd) = refs[n_band : n_band + 11]
    hist, grads_out, mean_out = refs[n_band + 11 : n_band + 14]
    (
        bands, band_sems, zf, p1, zj, p2, z2, p3, p4, h4, truth, mean_split,
        gs, gp4m, gj, gp3m, zg3, gp2m, zg2, gp1m, hi_pos, lo_pos,
        acc_up, acc_down, acc_mid, acc_in, acc_head,
    ) = refs[n_band + 14 :]
    many = n_band > 4
    me = lax.axis_index("band")
    cell_count = float(rows * lon_count)

    copies = [
        pltpu.make_async_copy(pays[k].at[pl.ds(3 * n_blocks, 8)], bands.at[k], band_sems.at[k])
        for k in range(1, n_band)
    ]
    for copy in copies:
        copy.start()
    for edge in (0, rows + 1):
        zf[edge] = jnp.zeros((32, half), BF16)
        zj[edge] = jnp.zeros((256, half), BF16)
        gs[edge] = jnp.zeros((128, half), BF16)
        gp4m[edge] = jnp.zeros((64, half), BF16)
        gp1m[edge] = jnp.zeros((64, half), BF16)
    for edge in (0, coarse + 1):
        zg2[edge] = jnp.zeros((96, half), BF16)
        gp2m[edge] = jnp.zeros((32, half), BF16)
    for edge in (0, coarse // 2 + 1):
        for par in range(2):
            z2[par, edge] = jnp.zeros((96, half), BF16)
            zg3[par, edge] = jnp.zeros((96, half), BF16)
            gp3m[par, edge] = jnp.zeros((32, half), BF16)
    fine_iota = iota((2 * LANES, 2 * LANES), 0)
    part_iota = iota((2 * LANES, 2 * LANES), 1)
    parting = (fine_iota == 2 * (part_iota % LANES) + part_iota // LANES).astype(F32).astype(BF16)
    chunks = window // (2 * LANES)
    for source in range(n_band):
        at = me ^ source
        pieces = []
        for chunk in range(2):
            if chunk < chunks:
                tiles = [
                    pays[source][
                        3 * n_blocks + 8 + (2 * chunk + t) * ROWS_BAND : 3 * n_blocks + 8 + (2 * chunk + t + 1) * ROWS_BAND
                    ]
                    for t in range(2)
                ]
                pieces.append(jnp.concatenate(tiles, axis=1))
            else:
                pieces.append(jnp.zeros((ROWS_BAND, 2 * LANES), F32))
        stacked = jnp.concatenate(split_three(jnp.concatenate(pieces, axis=0)) + (jnp.zeros((8, 2 * LANES), F32),), axis=0)
        parted = dot(stacked.astype(BF16), parting)
        parted = parted[0:8] + parted[8:16] + parted[16:24]
        for chunk in range(chunks):
            for phase in range(2):
                truth[at, phase * 4 : phase * 4 + 4, chunk * LANES : (chunk + 1) * LANES] = parted[
                    chunk * 4 : chunk * 4 + 4, phase * LANES : (phase + 1) * LANES
                ]

    for copy in copies:
        copy.wait()
    scales = [bands[1, 1, k] for k in range(4)]
    for source in range(1, n_band):
        station_sums(
            own, lon_count, n_blocks, 4 if many else n_blocks, me, pays[source], bands.at[source], scales,
            hist, hi_pos.at[source], lo_pos.at[source],
        )

    eight = 8 * n_band
    chunks = half // LANES
    sub = iota((8, 1), 0)
    per_scale = []
    for scale in range(4):
        stacked = []
        for chunk in range(chunks):
            tiles = [
                hist[:, (2 * chunk + t) * 32 + 8 * scale : (2 * chunk + t) * 32 + 8 * scale + 8, :].reshape(eight, LANES)
                for t in range(4)
            ]
            stacked.append(jnp.concatenate(tiles, axis=1))
        cells = jnp.concatenate(stacked, axis=0)
        high = cells.astype(BF16)
        low = (cells - high.astype(F32)).astype(BF16)
        both = dot(jnp.concatenate([high, low], axis=0), table[scale])
        total = both[: chunks * eight] + both[chunks * eight :]
        below = pltpu.roll(total, 1, 0)
        density = jnp.where(iota((chunks * eight, 1), 0) % 2 == 0, total, below)
        per_scale.append(total / (1.0 + density))

    def phase_rows(phase):
        lines = []
        for band in range(n_band):
            parts = [
                jnp.concatenate(
                    [
                        per_scale[scale][
                            chunk * eight + 8 * band : chunk * eight + 8 * band + 8,
                            phase * LANES : (phase + 1) * LANES,
                        ]
                        for chunk in range(chunks)
                    ],
                    axis=1,
                )
                for scale in range(4)
            ]
            for row in range(ROWS_BAND):
                line = None
                for scale in range(4):
                    turn = (2 * scale - 2 * row) % 8
                    moved = pltpu.roll(parts[scale], turn, 0) if turn else parts[scale]
                    line = moved if line is None else jnp.where(sub // 2 == scale, moved, line)
                lines.append(line)
        return jnp.concatenate(lines, axis=0)

    even, odd = phase_rows(0), phase_rows(1)
    odd_before = rolled(odd, 1)
    even_after = rolled(even, -1)
    for row in range(rows):
        pick = slice(row * 8, row * 8 + 8)
        zf[row + 1] = jnp.concatenate(
            [odd_before[pick], even[pick], odd[pick], even_after[pick]], axis=0
        ).astype(BF16)

    def first(group):
        pre = dot(w1[...], zf[pl.ds(4 * group, 6)].reshape(192, half))
        for out in range(4):
            row = 4 * group + out
            hidden, p1[row] = silu_and_slope(pre[64 * out : 64 * out + 64])
            zj[row + 1, 128:256, :] = four_shifts(hidden[:32], hidden[32:]).astype(BF16)

    looped(n_band, 1 if many else n_band, first)

    def second(index):
        pre = dot(wd[...], zj[pl.ds(4 * index, 6), 128:256, :].reshape(768, half))
        for par in range(2):
            row = 2 * index + par
            hidden, p2[row] = silu_and_slope(pre[32 * par : 32 * par + 32])
            z2[par, index + 1] = three_shifts(hidden, 2).astype(BF16)

    looped(coarse // 2, 4 if many else coarse // 2, second)

    def third(group):
        for par in range(2):
            pre = dot(wm[...], z2[par, pl.ds(4 * group, 6)].reshape(576, half))
            for out in range(4):
                row = 2 * (4 * group + out) + par
                hidden, p3[row] = silu_and_slope(pre[32 * out : 32 * out + 32])
                wide = four_shifts(hidden, hidden).astype(BF16)
                zj[2 * row + 1, 0:128, :] = wide
                zj[2 * row + 2, 0:128, :] = wide

    looped(coarse // 8, 1, third)

    def fourth(pair):
        pre = dot(wu[...], zj[pl.ds(2 * pair, 4)].reshape(1024, half))
        for out in range(2):
            row = 2 * pair + out
            hidden, p4[row] = silu_and_slope(pre[64 * out : 64 * out + 64])
            h4[row] = hidden.astype(BF16)

    looped(rows // 2, 2 if many else rows // 2, fourth)

    own_cells = jnp.clip(lon_count - me * own, 0, own) // 2
    place = iota((1, half), 1)
    mask = ((place >= HALO // 2) & (place < HALO // 2 + own_cells)).astype(F32)
    acc_head[...] = jnp.zeros_like(acc_head)

    def head(group):
        hidden = h4[pl.ds(4 * group, 4)].reshape(256, half)
        out = dot(wh[...], hidden)
        mean = out[:8]
        raw = out[8:]
        decay = jnp.exp(-jnp.abs(raw))
        noise = 0.1 + (jnp.maximum(raw, 0.0) + jnp.log1p(decay))
        error = (mean - truth[group]) / noise
        weight = 1.0 / (noise * cell_count)
        grad_mean = error * weight
        grad_raw = (1.0 - error * error) * weight * sigmoid(raw)
        grad_out = jnp.concatenate([grad_mean, grad_raw], axis=0)
        grad_bf = grad_out.astype(BF16)
        acc_head[...] += dot_lanes((grad_out * mask).astype(BF16), hidden)
        back = dot(wht[...], grad_bf)
        grad = back * p4[pl.ds(4 * group, 4)].reshape(256, half)
        for row in range(4):
            mine = grad[row * 64 : row * 64 + 64]
            gp4m[4 * group + row + 1] = (mine * mask).astype(BF16)
            gs[4 * group + row + 1] = four_shifts(mine[:32], mine[32:]).astype(BF16)
        parts = split_three(jnp.concatenate([mean[0:4], mean[4:8]], axis=1))
        mean_split[group] = jnp.concatenate(
            parts + (jnp.zeros((4, 2 * half), F32),), axis=0
        ).astype(BF16)

    looped(n_band, 1 if many else n_band, head)

    target = iota((2 * half, own), 1) + HALO
    origin = iota((2 * half, own), 0)
    joining = (target == 2 * (origin % half) + origin // half).astype(F32).astype(BF16)
    joined = dot(mean_split[...].reshape(16 * n_band, 2 * half), joining)
    for band in range(n_band):
        four = joined[16 * band : 16 * band + 8] + joined[16 * band + 8 : 16 * band + 16]
        four = four[0:4] + four[4:8]
        for tile in range(own_tiles):
            mean_out[band, tile] = four[:, tile * LANES : (tile + 1) * LANES]

    def join_back(index):
        for par in range(2):
            row = 2 * index + par
            back = dot(wf[...], gs[pl.ds(2 * row, 4)].reshape(512, half)).astype(BF16)
            total = None
            for side in range(2):
                mine = back[128 * side : 128 * side + 128]
                gj[2 * row + side] = mine[64:]
                up = mine[:64].astype(F32)
                part = up[:32] + up[32:]
                total = part if total is None else total + part
            grad = total * p3[row]
            gp3m[par, index + 1] = (grad * mask).astype(BF16)
            zg3[par, index + 1] = three_shifts(grad, 2).astype(BF16)

    looped(coarse // 2, 2 if many else coarse // 2, join_back)

    def mid_back(group):
        for par in range(2):
            back = dot(wmf[...], zg3[par, pl.ds(4 * group, 6)].reshape(576, half))
            for out in range(4):
                row = 2 * (4 * group + out) + par
                grad = back[32 * out : 32 * out + 32] * p2[row]
                gp2m[row + 1] = (grad * mask).astype(BF16)
                zg2[row + 1] = three_shifts(grad, 1).astype(BF16)

    looped(coarse // 8, 1, mid_back)

    def down_back(pair):
        back = dot(wbd[...], zg2[pl.ds(2 * pair, 4)].reshape(384, half))
        for out in range(4):
            fine = 4 * pair + out
            grad = (back[64 * out : 64 * out + 64] + gj[fine].astype(F32)) * p1[fine]
            gp1m[fine + 1] = (grad * mask).astype(BF16)

    looped(coarse // 2, 2 if many else coarse // 2, down_back)

    acc_up[...] = jnp.zeros_like(acc_up)
    acc_down[...] = jnp.zeros_like(acc_down)
    acc_mid[...] = jnp.zeros_like(acc_mid)
    acc_in[...] = jnp.zeros_like(acc_in)

    def weights_fine(row):
        acc_up[...] += dot_lanes(gp4m[pl.ds(row, 3)].reshape(192, half), zj[row + 1])
        acc_in[...] += dot_lanes(zf[row + 1], gp1m[pl.ds(row, 3)].reshape(192, half))

    looped(rows, 4 if many else rows, weights_fine)

    def weights_coarse(index):
        for par in range(2):
            row = 2 * index + par
            acc_mid[...] += dot_lanes(gp3m[par, pl.ds(index, 3)].reshape(96, half), z2[par, index + 1])
            acc_down[...] += dot_lanes(
                gp2m[pl.ds(row, 3)].reshape(96, half),
                zj[pl.ds(2 * row + 1, 2), 128:256, :].reshape(256, half),
            )

    looped(coarse // 2, 4 if many else coarse // 2, weights_coarse)

    up = acc_up[...]
    for step in range(3):
        first_up, second_up = up[64 * step : 64 * step + 32], up[64 * step + 32 : 64 * step + 64]
        for part in range(2):
            cols = slice(128 * part, 128 * part + 128)
            grads_out[96 * part + 32 * step : 96 * part + 32 * step + 32, :] = first_up[:, cols] + rolled(
                second_up[:, cols], -32
            )
    mid = acc_mid[...]
    grads_out[0:96, 96:128] = mid[:, 0:32]
    grads_out[96:192, 96:128] = mid[:, 32:64]
    down = acc_down[...]
    for tap, (step, side) in enumerate(((2, 1), (1, 0), (1, 1), (0, 0))):
        grads_out[192 + 32 * tap : 224 + 32 * tap, :] = down[
            32 * step : 32 * step + 32, 128 * side : 128 * side + 128
        ]
    inner = acc_in[...]
    for step in range(3):
        grads_out[320:344, 32 * step : 32 * step + 32] = (
            inner[0:24, 64 * step : 64 * step + 32] + inner[8:32, 64 * step + 32 : 64 * step + 64]
        )
    for part in range(4):
        grads_out[344:368, 32 * part : 32 * part + 32] = mid[24 * part : 24 * part + 24, 64:96]
    grads_out[320:344, 96:128] = jnp.zeros((24, 32), F32)
    grads_out[368:384] = jnp.zeros((16, LANES), F32)
    k_index = iota((16, 256), 0) % 8
    c_index = iota((16, 256), 1) // 32
    same = (k_index % 4 == c_index // 2) & (k_index // 4 == c_index % 2)
    heads = jnp.where(same, acc_head[...], 0.0)
    for kind in range(2):
        line = jnp.sum(heads[8 * kind : 8 * kind + 8], axis=0, keepdims=True)
        line = line[:, :128] + line[:, 128:]
        line = line + rolled(line, 64)
        line = line + rolled(line, 32)
        grads_out[320 + kind : 321 + kind, 96:128] = line[:, 96:128]


def unpack_kernel(sizes, *refs):
    n_band, own, lon_count = sizes
    low, high = refs[0], refs[1]
    means = refs[2 : 2 + n_band]
    mean_out, grad_in, grad_down, grad_mid, grad_up, grad_head, wide = refs[2 + n_band :]
    me = lax.axis_index("band")
    core = lax.rem(lax.axis_index("group"), 2)
    own_tiles = own // LANES
    first = jnp.where(core == 0, low[...], high[...])
    second = jnp.where(core == 0, high[...], low[...])
    part_a, part_b = first[0:96], first[96:192]
    down, inner, folded = second[0:128], second[128:152], second[152:176]
    last = jnp.concatenate([rolled(folded, -32 * part) for part in range(4)], axis=0)
    lane = iota((96, LANES), 1)
    mids = (rolled(part_a, -96), rolled(part_b, -96), last)
    for tap_col in range(3):
        ups = jnp.where(lane < 32, rolled(part_a, -32 * tap_col), rolled(part_b, 32 - 32 * tap_col))
        for tap_row in range(3):
            at = slice(32 * (2 - tap_row), 32 * (2 - tap_row) + 32)
            grad_up[tap_row, tap_col] = ups[at, 0:64]
            grad_mid[tap_row, tap_col] = mids[tap_col][at, 0:32]
    for tap_row in range(3):
        ins = rolled(inner, -32 * (2 - tap_row))
        for tap_col in range(3):
            grad_in[tap_row, tap_col] = ins[8 * tap_col : 8 * tap_col + 8, 0:32]
    for tap_col in range(4):
        downs = rolled(down, -32 * tap_col)
        for tap_row in range(4):
            grad_down[tap_row, tap_col] = downs[32 * tap_row : 32 * tap_row + 32, 0:32]
    grad_head[...] = rolled(inner[0:8], -96)[0:2, 0:32]
    for shift in range(n_band):
        origin = lax.rem(me - shift + n_band, n_band)
        for tile in range(own_tiles):
            at = pl.multiple_of((origin * own_tiles + tile) * LANES, LANES)
            wide[:, pl.ds(at, LANES)] = means[shift][tile]
    mean_out[0] = wide[:, 0:lon_count]


def swapped(values, axis, count, bits):
    return lax.ppermute(values, axis, [(i, i ^ bits) for i in range(count)])


def shifted(values, axis, count, shift):
    return lax.ppermute(values, axis, [(i, (i + shift) % count) for i in range(count)])


def reduced(grads, mean_tiles, n_band, n_group):
    group = lax.axis_index("group")
    band = lax.axis_index("band")
    core, side = group % 2, (group // 2) % 2
    half = grads.shape[0] // 2
    mine = lax.dynamic_slice_in_dim(grads, core * half, half, 0)
    theirs = lax.dynamic_slice_in_dim(grads, (1 - core) * half, half, 0)
    total = mine + swapped(theirs, "group", n_group, 1)
    share = half // 2
    kept = lax.dynamic_slice_in_dim(total, side * share, share, 0)
    other = lax.dynamic_slice_in_dim(total, (1 - side) * share, share, 0)
    got = [swapped(other if k % 2 else kept, "group", n_group, 2 * k) for k in range(1, n_group // 2)]
    for piece in got:
        kept = kept + piece
    means = [lax.dynamic_index_in_dim(mean_tiles, band, 0, keepdims=False)]
    arrived = []
    for k in range(1, n_band):
        target = lax.rem(band + k, n_band)
        sent = jnp.concatenate([kept, lax.dynamic_index_in_dim(mean_tiles, target, 0, keepdims=False)])
        arrived.append(shifted(sent, "band", n_band, k))
    for piece in arrived:
        kept = kept + piece[:share]
        means.append(piece[share:])
    other = swapped(kept, "group", n_group, 2)
    whole = jnp.where(side == 0, jnp.concatenate([kept, other]), jnp.concatenate([other, kept]))
    return whole, swapped(whole, "group", n_group, 1), means


def vmem(*shape, dtype=BF16):
    return pltpu.VMEM(shape, dtype)


def local(
    station_rows,
    station_lons,
    station_obs,
    station_live,
    block_band,
    truth_field,
    length_scales,
    w_in,
    w_down,
    w_mid,
    w_up,
    w_head,
):
    n_band = lax.axis_size("band")
    n_group = lax.axis_size("group")
    n_blocks = station_rows.shape[1]
    lon_count = truth_field.shape[2]
    own_tiles = -(-(-(-lon_count // LANES)) // n_band)
    own = own_tiles * LANES
    window = own + 2 * HALO
    half = window // 2
    rows = ROWS_BAND * n_band
    coarse = rows // 2
    hist_tiles = (window + 2 * REACH) // LANES

    sizes = (n_band, n_blocks, own, lon_count)
    pay_rows = 3 * n_blocks + 8 + -(-(window // LANES) * ROWS_BAND // 8) * 8
    wide_lanes = (n_band * own_tiles + 1) * LANES
    in_vmem = pl.BlockSpec(memory_space=pltpu.VMEM)
    in_hbm = pl.BlockSpec(memory_space=pltpu.HBM)

    def in_place(arg):
        return pltpu.with_memory_space_constraint(arg, pltpu.HBM)

    def shaped(*shape, dtype=BF16):
        return jax.ShapeDtypeStruct(shape, dtype)

    arrays = (
        station_rows, station_lons, station_obs, station_live, block_band.reshape(1, n_blocks), truth_field,
        length_scales.reshape(1, 4),
    )
    packed = pl.pallas_call(
        functools.partial(pack_kernel, sizes),
        out_shape=(shaped(pay_rows, LANES, dtype=F32),) * n_band,
        in_specs=[in_hbm] * 7,
        out_specs=(in_vmem,) * n_band,
        scratch_shapes=[vmem(ROWS_BAND, wide_lanes, dtype=F32)]
        + [vmem(*arg.shape, dtype=arg.dtype) for arg in arrays]
        + [pltpu.SemaphoreType.DMA((7,))],
        compiler_params=pltpu.CompilerParams(vmem_limit_bytes=8 * 1024 * 1024),
    )(*[in_place(arg) for arg in arrays])
    pays = [packed[0]] + [swapped(packed[k], "band", n_band, k) for k in range(1, n_band)]

    hist_shape = (n_band, hist_tiles * 32, LANES)
    weights = (jnp.transpose(w_in, (0, 1, 3, 2)), w_down, w_mid, w_up, w_head)
    early = pl.pallas_call(
        functools.partial(early_kernel, sizes),
        out_shape=(
            shaped(*hist_shape, dtype=F32),
            shaped(4, 4 * LANES, 2 * LANES),
            shaped(256, 192),
            shaped(64, 768),
            shaped(128, 576),
            shaped(128, 1024),
            shaped(16, 256),
            shaped(256, 16),
            shaped(256, 512),
            shaped(128, 576),
            shaped(256, 384),
        ),
        in_specs=[in_vmem] + [in_hbm] * 5,
        out_specs=(in_vmem,) * 11,
        scratch_shapes=[
            pltpu.SMEM((8, LANES), F32),
            vmem(n_blocks, LANES, dtype=F32),
            vmem(n_blocks, LANES, dtype=F32),
            vmem(256, 256, dtype=F32),
            vmem(32, 512, dtype=F32),
            vmem(128, 576, dtype=F32),
            vmem(64, 768, dtype=F32),
            vmem(384, 128, dtype=F32),
            vmem(640, 128, dtype=F32),
            vmem(384, 256, dtype=F32),
        ]
        + [vmem(*arg.shape) for arg in weights]
        + [pltpu.SemaphoreType.DMA((6,))],
        compiler_params=pltpu.CompilerParams(vmem_limit_bytes=16 * 1024 * 1024),
        cost_estimate=pl.CostEstimate(flops=200_000_000, bytes_accessed=2_000_000, transcendentals=700_000),
    )(packed[0], *[in_place(arg) for arg in weights])

    _, grads, mean_tiles = pl.pallas_call(
        functools.partial(network_kernel, sizes),
        out_shape=(
            shaped(*hist_shape, dtype=F32),
            shaped(384, LANES, dtype=F32),
            shaped(n_band, own_tiles, ROWS_BAND, LANES, dtype=F32),
        ),
        in_specs=[in_vmem] * (n_band + 11),
        out_specs=(in_vmem, in_vmem, in_vmem),
        input_output_aliases={n_band: 0},
        scratch_shapes=[
            pltpu.SMEM((n_band, 8, LANES), F32),
            pltpu.SemaphoreType.DMA((n_band,)),
            vmem(rows + 2, 32, half),
            vmem(rows, 64, half, dtype=F32),
            vmem(rows + 2, 256, half),
            vmem(coarse, 32, half, dtype=F32),
            vmem(2, coarse // 2 + 2, 96, half),
            vmem(coarse, 32, half, dtype=F32),
            vmem(rows, 64, half, dtype=F32),
            vmem(rows, 64, half),
            vmem(n_band, 8, half, dtype=F32),
            vmem(n_band, 16, 2 * half),
            vmem(rows + 2, 128, half),
            vmem(rows + 2, 64, half),
            vmem(rows, 64, half),
            vmem(2, coarse // 2 + 2, 32, half),
            vmem(2, coarse // 2 + 2, 96, half),
            vmem(coarse + 2, 32, half),
            vmem(coarse + 2, 96, half),
            vmem(rows + 2, 64, half),
            vmem(n_band, n_blocks, LANES, dtype=F32),
            vmem(n_band, n_blocks, LANES, dtype=F32),
            vmem(192, 256, dtype=F32),
            vmem(96, 256, dtype=F32),
            vmem(96, 96, dtype=F32),
            vmem(32, 192, dtype=F32),
            vmem(16, 256, dtype=F32),
        ],
        compiler_params=pltpu.CompilerParams(vmem_limit_bytes=40 * 1024 * 1024),
        cost_estimate=pl.CostEstimate(flops=4_000_000_000, bytes_accessed=4_000_000, transcendentals=2_000_000),
    )(*pays, *early)

    low, high, means = reduced(grads, mean_tiles.reshape(n_band, own_tiles * ROWS_BAND, LANES), n_band, n_group)
    means = [piece.reshape(own_tiles, ROWS_BAND, LANES) for piece in means]
    outs = pl.pallas_call(
        functools.partial(unpack_kernel, (n_band, own, lon_count)),
        out_shape=(
            jax.ShapeDtypeStruct((1, ROWS_BAND, lon_count), F32),
            jax.ShapeDtypeStruct((3, 3, 8, 32), F32),
            jax.ShapeDtypeStruct((4, 4, 32, 32), F32),
            jax.ShapeDtypeStruct((3, 3, 32, 32), F32),
            jax.ShapeDtypeStruct((3, 3, 32, 64), F32),
            jax.ShapeDtypeStruct((2, 32), F32),
        ),
        in_specs=[in_vmem] * (2 + n_band),
        out_specs=(in_vmem,) * 6,
        scratch_shapes=[vmem(ROWS_BAND, n_band * own, dtype=F32)],
        compiler_params=pltpu.CompilerParams(vmem_limit_bytes=16 * 1024 * 1024),
    )(low, high, *means)
    return (outs[0], jnp.transpose(outs[1], (0, 1, 3, 2))) + tuple(outs[2:])


def solution(mesh):
    return jax.shard_map(
        local,
        mesh=mesh,
        in_specs=(
            P("group", "band", None),
            P("group", "band", None),
            P("group", "band", None),
            P("group", "band", None),
            P("group", "band", None),
            P("group", "band", None),
            P(),
            P(),
            P(),
            P(),
            P(),
            P(),
        ),
        out_specs=(P("group", "band", None), P(), P(), P(), P(), P()),
        check_vma=False,
    )
```

```python
import functools

import jax
import jax.numpy as jnp
from jax import lax
from jax.experimental import pallas as pl
from jax.experimental.pallas import tpu as pltpu
from jax.sharding import PartitionSpec as P

LANES = 128
HALO = 64
REACH = 128
ROWS_BAND = 4
FAR = -1.0e6
F32 = jnp.float32
BF16 = jnp.bfloat16


def looped(count, step, body):
    step = min(step, count)
    if count == step:
        for index in range(count):
            body(index)
    else:

        def turn(outer, carry):
            for inner in range(step):
                body(outer * step + inner)
            return carry

        lax.fori_loop(0, count // step, turn, 0)


def dot(first, second):
    return jnp.dot(first, second, preferred_element_type=F32)


def dot_lanes(first, second):
    return lax.dot_general(first, second, (((1,), (1,)), ((), ())), preferred_element_type=F32)


def iota(shape, dim):
    return lax.broadcasted_iota(jnp.int32, shape, dim)


def rolled(values, shift):
    width = values.shape[-1]
    return pltpu.roll(values, shift % width, values.ndim - 1)


def four_shifts(even, odd):
    return jnp.concatenate([rolled(odd, 1), even, odd, rolled(even, -1)], axis=0)


def three_shifts(values, width):
    return jnp.concatenate([rolled(values, width), values, rolled(values, -width)], axis=0)


def sigmoid(values):
    return 0.5 + 0.5 * jnp.tanh(0.5 * values)


def silu_and_slope(values):
    squash = sigmoid(values)
    hidden = values * squash
    return hidden, squash + hidden * (1.0 - squash)


def split_three(values):
    high = values.astype(BF16).astype(F32)
    rest = values - high
    middle = rest.astype(BF16).astype(F32)
    return high, middle, rest - middle


def station_sums(own, lon_count, n_blocks, step, me, pay, bands, scales, hist, hi_pos, lo_pos):
    hist_tiles = hist.shape[1] // 32
    start = (me * own - HALO - REACH).astype(F32)
    place = pay[n_blocks : 2 * n_blocks] - start
    place = jnp.where(place < 0.0, place + lon_count, place)
    place = jnp.where(place < 0.0, place + lon_count, place)
    place = jnp.where(place >= lon_count, place - lon_count, place)
    tile_of = jnp.floor(place * (1.0 / LANES))
    hi_pos[...] = tile_of
    lo_pos[...] = place - tile_of * LANES

    m_index = iota((32, 1), 0)
    row_of = ((m_index % 8) // 2).astype(F32)
    scale_of = m_index // 8
    kind_of = m_index % 2
    spread = jnp.where(
        scale_of == 0, scales[0], jnp.where(scale_of == 1, scales[1], jnp.where(scale_of == 2, scales[2], scales[3]))
    )
    rate = -0.5 / (spread * spread)
    lane_iota = iota((LANES, LANES), 0).astype(F32)

    def one_block(block):
        at_row = pay[pl.ds(block, 1), :]
        observed = pay[pl.ds(2 * n_blocks + block, 1), :]
        high = hi_pos[pl.ds(block, 1), :]
        low = lo_pos[pl.ds(block, 1), :]
        gap = row_of - at_row
        left = jnp.exp(gap * gap * rate) * jnp.where(kind_of == 0, 1.0, observed)
        spread_left = jnp.concatenate(
            [jnp.where(high == float(tile), left, 0.0) for tile in range(hist_tiles)], axis=0
        ).astype(BF16)
        one_hot = jnp.where(lane_iota == low, 1.0, 0.0).astype(BF16)
        band = bands[0, block].astype(jnp.int32)
        hist[band] = hist[band] + dot_lanes(spread_left, one_hot)

    looped(n_blocks, step, one_block)


def pack_kernel(sizes, *refs):
    n_band, n_blocks, own, lon_count = sizes
    pays = refs[7 : 7 + n_band]
    wide = refs[7 + n_band]
    held, sems = refs[8 + n_band : 15 + n_band], refs[15 + n_band]
    copies = [pltpu.make_async_copy(refs[k], held[k], sems.at[k]) for k in range(7)]
    for copy in copies:
        copy.start()
    for copy in copies:
        copy.wait()
    rows, lons, obs, live, block_band, field, scales = held
    me = lax.axis_index("band")
    at_row = rows[0].astype(F32)
    lon = jnp.where(live[0] > 0, lons[0].astype(F32), FAR)
    total = wide.shape[1]
    wide[:, 0:HALO] = field[0, :, lon_count - HALO : lon_count]
    wide[:, HALO : HALO + lon_count] = field[0]
    wide[:, HALO + lon_count : total] = field[0, :, 0 : total - HALO - lon_count]
    for shift in range(n_band):
        pay = pays[shift]
        pay[0:n_blocks] = at_row
        pay[n_blocks : 2 * n_blocks] = lon
        pay[2 * n_blocks : 3 * n_blocks] = obs[0]
        pay[3 * n_blocks : 3 * n_blocks + 8] = jnp.zeros((8, LANES), F32)
        pay[3 * n_blocks : 3 * n_blocks + 1, 0:n_blocks] = block_band[...].astype(F32)
        pay[3 * n_blocks + 1 : 3 * n_blocks + 2, 0:4] = scales[...]
        target = me ^ shift
        for tile in range((own + 2 * HALO) // LANES):
            at = pl.multiple_of(target * own + tile * LANES, LANES)
            first = 3 * n_blocks + 8 + ROWS_BAND * tile
            pay[first : first + ROWS_BAND] = wide[:, pl.ds(at, LANES)]


def early_kernel(sizes, *refs):
    n_band, n_blocks, own, lon_count = sizes
    pay = refs[0]
    hist, table, w1, wd, wm, wu, wh, wht, wf, wmf, wbd = refs[6:17]
    bands, hi_pos, lo_pos, t1, td, tm, tu, tf, tmf, tbd = refs[17:27]
    held, sems = refs[27:32], refs[32]
    me = lax.axis_index("band")
    band_copy = pltpu.make_async_copy(pay.at[pl.ds(3 * n_blocks, 8)], bands, sems.at[5])
    band_copy.start()
    copies = [pltpu.make_async_copy(refs[1 + k], held[k], sems.at[k]) for k in range(5)]
    for copy in copies:
        copy.start()
    place_in = iota((4 * LANES, 2 * LANES), 0)
    place_out = iota((4 * LANES, 2 * LANES), 1)
    distance = (place_in - (REACH + 2 * (place_out % LANES) + place_out // LANES)).astype(F32)
    squared = distance * distance
    band_copy.wait()
    scales = [bands[1, k] for k in range(4)]
    hist[...] = jnp.zeros_like(hist)
    step = n_blocks if n_band <= 4 else 4
    station_sums(own, lon_count, n_blocks, step, me, pay, bands, scales, hist, hi_pos, lo_pos)
    for scale in range(4):
        table[scale] = jnp.exp(squared * (-0.5 / (scales[scale] * scales[scale]))).astype(BF16)

    for copy in copies:
        copy.wait()
    w_in, w_down, w_mid, w_up, w_head = held
    for held in (t1, tm, tu, tf, tmf, tbd):
        held[...] = jnp.zeros_like(held)
    for row in range(3):
        for col in range(3):
            inner = w_in[row, col].astype(F32)
            mid = w_mid[row, col].astype(F32)
            up = w_up[row, col].astype(F32)
            back = (2 - row) * 3 + 2 - col
            for out in range(4):
                at = out * 96 + (row * 3 + col) * 32
                tm[out * 32 : out * 32 + 32, at : at + 32] = mid
                at = out * 96 + back * 32
                tmf[at : at + 32, out * 32 : out * 32 + 32] = mid
            for phase in range(2):
                for out in range(4):
                    at = (out + row) * 32 + (phase + col) * 8
                    to = out * 64 + phase * 32
                    t1[at : at + 8, to : to + 32] = inner
                for part in range(2):
                    cols = slice(part * 32, part * 32 + 32)
                    at = (row * 2 + part) * 128 + (phase + col) * 32
                    tu[phase * 32 : phase * 32 + 32, at : at + 32] = up[:, cols]
                    at = (2 - row) * 128 + (phase + 2 - col) * 32
                    to = part * 64 + phase * 32
                    tf[at : at + 32, to : to + 32] = up[:, cols]
    sides = (((1, 0), (3, -1)), ((0, 1), (2, 0)))
    for row in range(4):
        for col in range(4):
            td[:, (row * 4 + col) * 32 : (row * 4 + col) * 32 + 32] = w_down[row, col].astype(F32)
    for side in range(2):
        for phase in range(2):
            for row, row_shift in sides[side]:
                for col, col_shift in sides[phase]:
                    for out in range(2):
                        at = (out + row_shift + 1) * 96 + (col_shift + 1) * 32
                        to = out * 128 + (side * 2 + phase) * 32
                        tbd[at : at + 32, to : to + 32] = w_down[row, col].astype(F32)

    def two_rows(one, shift):
        empty = jnp.zeros((one.shape[0], shift), F32)
        return jnp.concatenate(
            [jnp.concatenate([one, empty], axis=1), jnp.concatenate([empty, one], axis=1)], axis=0
        ).astype(BF16)

    w1[...] = t1[...].T[:, 0:192].astype(BF16)
    wd[...] = two_rows(td[...], 256)
    wm[...] = tm[...].astype(BF16)
    wu[...] = two_rows(tu[...], 256)
    wf[...] = two_rows(tf[...].T, 128)
    wmf[...] = tmf[...].T[:, 0:576].astype(BF16)
    wbd[...] = tbd[...].T.astype(BF16)
    heads = w_head[...].astype(F32)
    heads = jnp.concatenate([heads, jnp.zeros((6, 32), F32)], axis=0)
    heads = jnp.concatenate([heads, jnp.zeros((8, 96), F32)], axis=1)
    heads = heads + rolled(heads, 32)
    heads = heads + rolled(heads, 64)
    heads = jnp.concatenate([heads, heads], axis=1)
    k_index = iota((128, 256), 0)
    c_index = iota((128, 256), 1) // 32
    same = (k_index % 4 == c_index // 2) & ((k_index // 4) % 2 == c_index % 2) & (k_index < 16)
    full = jnp.where(same, jnp.where(k_index < 8, heads[0:1], heads[1:2]), 0.0)
    wh[...] = full[0:16].astype(BF16)
    wht[...] = full.T[:, 0:16].astype(BF16)


def network_kernel(sizes, *refs):
    n_band, n_blocks, own, lon_count = sizes
    window = own + 2 * HALO
    half = window // 2
    rows = ROWS_BAND * n_band
    coarse = rows // 2
    own_tiles = own // LANES
    pays = refs[:n_band]
    (hist_own, table, w1, wd, wm, wu, wh, wht, wf, wmf, wbd) = refs[n_band : n_band + 11]
    hist, grads_out, mean_out = refs[n_band + 11 : n_band + 14]
    (
        bands, band_sems, zf, p1, zj, p2, z2, p3, p4, h4, truth, mean_split,
        gs, gp4m, gj, gp3m, zg3, gp2m, zg2, gp1m, hi_pos, lo_pos,
        acc_up, acc_down, acc_mid, acc_in, acc_head,
    ) = refs[n_band + 14 :]
    many = n_band > 4
    me = lax.axis_index("band")
    cell_count = float(rows * lon_count)

    copies = [
        pltpu.make_async_copy(pays[k].at[pl.ds(3 * n_blocks, 8)], bands.at[k], band_sems.at[k])
        for k in range(1, n_band)
    ]
    for copy in copies:
        copy.start()
    for edge in (0, rows + 1):
        zf[edge] = jnp.zeros((32, half), BF16)
        zj[edge] = jnp.zeros((256, half), BF16)
        gs[edge] = jnp.zeros((128, half), BF16)
        gp4m[edge] = jnp.zeros((64, half), BF16)
        gp1m[edge] = jnp.zeros((64, half), BF16)
    for edge in (0, coarse + 1):
        zg2[edge] = jnp.zeros((96, half), BF16)
        gp2m[edge] = jnp.zeros((32, half), BF16)
    for edge in (0, coarse // 2 + 1):
        for par in range(2):
            z2[par, edge] = jnp.zeros((96, half), BF16)
            zg3[par, edge] = jnp.zeros((96, half), BF16)
            gp3m[par, edge] = jnp.zeros((32, half), BF16)
    fine_iota = iota((2 * LANES, 2 * LANES), 0)
    part_iota = iota((2 * LANES, 2 * LANES), 1)
    parting = (fine_iota == 2 * (part_iota % LANES) + part_iota // LANES).astype(F32).astype(BF16)
    chunks = window // (2 * LANES)
    for source in range(n_band):
        at = me ^ source
        pieces = []
        for chunk in range(2):
            if chunk < chunks:
                tiles = [
                    pays[source][
                        3 * n_blocks + 8 + (2 * chunk + t) * ROWS_BAND : 3 * n_blocks + 8 + (2 * chunk + t + 1) * ROWS_BAND
                    ]
                    for t in range(2)
                ]
                pieces.append(jnp.concatenate(tiles, axis=1))
            else:
                pieces.append(jnp.zeros((ROWS_BAND, 2 * LANES), F32))
        stacked = jnp.concatenate(split_three(jnp.concatenate(pieces, axis=0)) + (jnp.zeros((8, 2 * LANES), F32),), axis=0)
        parted = dot(stacked.astype(BF16), parting)
        parted = parted[0:8] + parted[8:16] + parted[16:24]
        for chunk in range(chunks):
            for phase in range(2):
                truth[at, phase * 4 : phase * 4 + 4, chunk * LANES : (chunk + 1) * LANES] = parted[
                    chunk * 4 : chunk * 4 + 4, phase * LANES : (phase + 1) * LANES
                ]

    for copy in copies:
        copy.wait()
    scales = [bands[1, 1, k] for k in range(4)]
    for source in range(1, n_band):
        station_sums(
            own, lon_count, n_blocks, 4 if many else n_blocks, me, pays[source], bands.at[source], scales,
            hist, hi_pos.at[source], lo_pos.at[source],
        )

    eight = 8 * n_band
    chunks = half // LANES
    sub = iota((8, 1), 0)
    per_scale = []
    for scale in range(4):
        stacked = []
        for chunk in range(chunks):
            tiles = [
                hist[:, (2 * chunk + t) * 32 + 8 * scale : (2 * chunk + t) * 32 + 8 * scale + 8, :].reshape(eight, LANES)
                for t in range(4)
            ]
            stacked.append(jnp.concatenate(tiles, axis=1))
        cells = jnp.concatenate(stacked, axis=0)
        high = cells.astype(BF16)
        low = (cells - high.astype(F32)).astype(BF16)
        both = dot(jnp.concatenate([high, low], axis=0), table[scale])
        total = both[: chunks * eight] + both[chunks * eight :]
        below = pltpu.roll(total, 1, 0)
        density = jnp.where(iota((chunks * eight, 1), 0) % 2 == 0, total, below)
        per_scale.append(total / (1.0 + density))

    def phase_rows(phase):
        lines = []
        for band in range(n_band):
            parts = [
                jnp.concatenate(
                    [
                        per_scale[scale][
                            chunk * eight + 8 * band : chunk * eight + 8 * band + 8,
                            phase * LANES : (phase + 1) * LANES,
                        ]
                        for chunk in range(chunks)
                    ],
                    axis=1,
                )
                for scale in range(4)
            ]
            for row in range(ROWS_BAND):
                line = None
                for scale in range(4):
                    turn = (2 * scale - 2 * row) % 8
                    moved = pltpu.roll(parts[scale], turn, 0) if turn else parts[scale]
                    line = moved if line is None else jnp.where(sub // 2 == scale, moved, line)
                lines.append(line)
        return jnp.concatenate(lines, axis=0)

    even, odd = phase_rows(0), phase_rows(1)
    odd_before = rolled(odd, 1)
    even_after = rolled(even, -1)
    for row in range(rows):
        pick = slice(row * 8, row * 8 + 8)
        zf[row + 1] = jnp.concatenate(
            [odd_before[pick], even[pick], odd[pick], even_after[pick]], axis=0
        ).astype(BF16)

    def first(group):
        pre = dot(w1[...], zf[pl.ds(4 * group, 6)].reshape(192, half))
        for out in range(4):
            row = 4 * group + out
            hidden, p1[row] = silu_and_slope(pre[64 * out : 64 * out + 64])
            zj[row + 1, 128:256, :] = four_shifts(hidden[:32], hidden[32:]).astype(BF16)

    looped(n_band, 1 if many else n_band, first)

    def second(index):
        pre = dot(wd[...], zj[pl.ds(4 * index, 6), 128:256, :].reshape(768, half))
        for par in range(2):
            row = 2 * index + par
            hidden, p2[row] = silu_and_slope(pre[32 * par : 32 * par + 32])
            z2[par, index + 1] = three_shifts(hidden, 2).astype(BF16)

    looped(coarse // 2, 4 if many else coarse // 2, second)

    def third(group):
        for par in range(2):
            pre = dot(wm[...], z2[par, pl.ds(4 * group, 6)].reshape(576, half))
            for out in range(4):
                row = 2 * (4 * group + out) + par
                hidden, p3[row] = silu_and_slope(pre[32 * out : 32 * out + 32])
                wide = four_shifts(hidden, hidden).astype(BF16)
                zj[2 * row + 1, 0:128, :] = wide
                zj[2 * row + 2, 0:128, :] = wide

    looped(coarse // 8, 1, third)

    def fourth(pair):
        pre = dot(wu[...], zj[pl.ds(2 * pair, 4)].reshape(1024, half))
        for out in range(2):
            row = 2 * pair + out
            hidden, p4[row] = silu_and_slope(pre[64 * out : 64 * out + 64])
            h4[row] = hidden.astype(BF16)

    looped(rows // 2, 2 if many else rows // 2, fourth)

    own_cells = jnp.clip(lon_count - me * own, 0, own) // 2
    place = iota((1, half), 1)
    mask = ((place >= HALO // 2) & (place < HALO // 2 + own_cells)).astype(F32)
    acc_head[...] = jnp.zeros_like(acc_head)

    def head(group):
        hidden = h4[pl.ds(4 * group, 4)].reshape(256, half)
        out = dot(wh[...], hidden)
        mean = out[:8]
        raw = out[8:]
        decay = jnp.exp(-jnp.abs(raw))
        noise = 0.1 + (jnp.maximum(raw, 0.0) + jnp.log1p(decay))
        error = (mean - truth[group]) / noise
        weight = 1.0 / (noise * cell_count)
        grad_mean = error * weight
        grad_raw = (1.0 - error * error) * weight * sigmoid(raw)
        grad_out = jnp.concatenate([grad_mean, grad_raw], axis=0)
        grad_bf = grad_out.astype(BF16)
        acc_head[...] += dot_lanes((grad_out * mask).astype(BF16), hidden)
        back = dot(wht[...], grad_bf)
        grad = back * p4[pl.ds(4 * group, 4)].reshape(256, half)
        for row in range(4):
            mine = grad[row * 64 : row * 64 + 64]
            gp4m[4 * group + row + 1] = (mine * mask).astype(BF16)
            gs[4 * group + row + 1] = four_shifts(mine[:32], mine[32:]).astype(BF16)
        parts = split_three(jnp.concatenate([mean[0:4], mean[4:8]], axis=1))
        mean_split[group] = jnp.concatenate(
            parts + (jnp.zeros((4, 2 * half), F32),), axis=0
        ).astype(BF16)

    looped(n_band, 1 if many else n_band, head)

    target = iota((2 * half, own), 1) + HALO
    origin = iota((2 * half, own), 0)
    joining = (target == 2 * (origin % half) + origin // half).astype(F32).astype(BF16)
    joined = dot(mean_split[...].reshape(16 * n_band, 2 * half), joining)
    for band in range(n_band):
        four = joined[16 * band : 16 * band + 8] + joined[16 * band + 8 : 16 * band + 16]
        four = four[0:4] + four[4:8]
        for tile in range(own_tiles):
            mean_out[band, tile] = four[:, tile * LANES : (tile + 1) * LANES]

    acc_up[...] = jnp.zeros_like(acc_up)
    acc_down[...] = jnp.zeros_like(acc_down)
    acc_mid[...] = jnp.zeros_like(acc_mid)
    acc_in[...] = jnp.zeros_like(acc_in)

    def join_back(index):
        for par in range(2):
            row = 2 * index + par
            back = dot(wf[...], gs[pl.ds(2 * row, 4)].reshape(512, half)).astype(BF16)
            total = None
            for side in range(2):
                mine = back[128 * side : 128 * side + 128]
                gj[2 * row + side] = mine[64:]
                up = mine[:64].astype(F32)
                part = up[:32] + up[32:]
                total = part if total is None else total + part
            grad = total * p3[row]
            gp3m[par, index + 1] = (grad * mask).astype(BF16)
            zg3[par, index + 1] = three_shifts(grad, 2).astype(BF16)

    looped(coarse // 2, 2 if many else coarse // 2, join_back)

    def weights_up(row):
        acc_up[...] += dot_lanes(gp4m[pl.ds(row, 3)].reshape(192, half), zj[row + 1])

    looped(rows, 4 if many else rows, weights_up)

    def mid_back(group):
        for par in range(2):
            back = dot(wmf[...], zg3[par, pl.ds(4 * group, 6)].reshape(576, half))
            for out in range(4):
                row = 2 * (4 * group + out) + par
                grad = back[32 * out : 32 * out + 32] * p2[row]
                gp2m[row + 1] = (grad * mask).astype(BF16)
                zg2[row + 1] = three_shifts(grad, 1).astype(BF16)

    looped(coarse // 8, 1, mid_back)

    def weights_mid(index):
        for par in range(2):
            acc_mid[...] += dot_lanes(gp3m[par, pl.ds(index, 3)].reshape(96, half), z2[par, index + 1])

    looped(coarse // 2, 4 if many else coarse // 2, weights_mid)

    def down_back(pair):
        back = dot(wbd[...], zg2[pl.ds(2 * pair, 4)].reshape(384, half))
        for out in range(4):
            fine = 4 * pair + out
            grad = (back[64 * out : 64 * out + 64] + gj[fine].astype(F32)) * p1[fine]
            gp1m[fine + 1] = (grad * mask).astype(BF16)

    looped(coarse // 2, 2 if many else coarse // 2, down_back)

    def weights_down(row):
        acc_down[...] += dot_lanes(
            gp2m[pl.ds(row, 3)].reshape(96, half),
            zj[pl.ds(2 * row + 1, 2), 128:256, :].reshape(256, half),
        )

    looped(coarse, 4 if many else coarse, weights_down)

    def weights_in(row):
        acc_in[...] += dot_lanes(zf[row + 1], gp1m[pl.ds(row, 3)].reshape(192, half))

    looped(rows, 4 if many else rows, weights_in)

    up = acc_up[...]
    for step in range(3):
        first_up, second_up = up[64 * step : 64 * step + 32], up[64 * step + 32 : 64 * step + 64]
        for part in range(2):
            cols = slice(128 * part, 128 * part + 128)
            grads_out[96 * part + 32 * step : 96 * part + 32 * step + 32, :] = first_up[:, cols] + rolled(
                second_up[:, cols], -32
            )
    mid = acc_mid[...]
    grads_out[0:96, 96:128] = mid[:, 0:32]
    grads_out[96:192, 96:128] = mid[:, 32:64]
    down = acc_down[...]
    for tap, (step, side) in enumerate(((2, 1), (1, 0), (1, 1), (0, 0))):
        grads_out[192 + 32 * tap : 224 + 32 * tap, :] = down[
            32 * step : 32 * step + 32, 128 * side : 128 * side + 128
        ]
    inner = acc_in[...]
    for step in range(3):
        grads_out[320:344, 32 * step : 32 * step + 32] = (
            inner[0:24, 64 * step : 64 * step + 32] + inner[8:32, 64 * step + 32 : 64 * step + 64]
        )
    for part in range(4):
        grads_out[344:368, 32 * part : 32 * part + 32] = mid[24 * part : 24 * part + 24, 64:96]
    grads_out[320:344, 96:128] = jnp.zeros((24, 32), F32)
    grads_out[368:384] = jnp.zeros((16, LANES), F32)
    k_index = iota((16, 256), 0) % 8
    c_index = iota((16, 256), 1) // 32
    same = (k_index % 4 == c_index // 2) & (k_index // 4 == c_index % 2)
    heads = jnp.where(same, acc_head[...], 0.0)
    for kind in range(2):
        line = jnp.sum(heads[8 * kind : 8 * kind + 8], axis=0, keepdims=True)
        line = line[:, :128] + line[:, 128:]
        line = line + rolled(line, 64)
        line = line + rolled(line, 32)
        grads_out[320 + kind : 321 + kind, 96:128] = line[:, 96:128]


def unpack_kernel(sizes, *refs):
    n_band, own, lon_count = sizes
    low, high = refs[0], refs[1]
    means = refs[2 : 2 + n_band]
    mean_out, grad_in, grad_down, grad_mid, grad_up, grad_head, wide = refs[2 + n_band :]
    me = lax.axis_index("band")
    core = lax.rem(lax.axis_index("group"), 2)
    own_tiles = own // LANES
    first = jnp.where(core == 0, low[...], high[...])
    second = jnp.where(core == 0, high[...], low[...])
    part_a, part_b = first[0:96], first[96:192]
    down, inner, folded = second[0:128], second[128:152], second[152:176]
    last = jnp.concatenate([rolled(folded, -32 * part) for part in range(4)], axis=0)
    lane = iota((96, LANES), 1)
    mids = (rolled(part_a, -96), rolled(part_b, -96), last)
    for tap_col in range(3):
        ups = jnp.where(lane < 32, rolled(part_a, -32 * tap_col), rolled(part_b, 32 - 32 * tap_col))
        for tap_row in range(3):
            at = slice(32 * (2 - tap_row), 32 * (2 - tap_row) + 32)
            grad_up[tap_row, tap_col] = ups[at, 0:64]
            grad_mid[tap_row, tap_col] = mids[tap_col][at, 0:32]
    for tap_row in range(3):
        ins = rolled(inner, -32 * (2 - tap_row))
        for tap_col in range(3):
            grad_in[tap_row, tap_col] = ins[8 * tap_col : 8 * tap_col + 8, 0:32]
    for tap_col in range(4):
        downs = rolled(down, -32 * tap_col)
        for tap_row in range(4):
            grad_down[tap_row, tap_col] = downs[32 * tap_row : 32 * tap_row + 32, 0:32]
    grad_head[...] = rolled(inner[0:8], -96)[0:2, 0:32]
    for shift in range(n_band):
        origin = lax.rem(me - shift + n_band, n_band)
        for tile in range(own_tiles):
            at = pl.multiple_of((origin * own_tiles + tile) * LANES, LANES)
            wide[:, pl.ds(at, LANES)] = means[shift][tile]
    mean_out[0] = wide[:, 0:lon_count]


def swapped(values, axis, count, bits):
    return lax.ppermute(values, axis, [(i, i ^ bits) for i in range(count)])


def shifted(values, axis, count, shift):
    return lax.ppermute(values, axis, [(i, (i + shift) % count) for i in range(count)])


def reduced(grads, mean_tiles, n_band, n_group):
    group = lax.axis_index("group")
    band = lax.axis_index("band")
    core, side = group % 2, (group // 2) % 2
    half = grads.shape[0] // 2
    mine = lax.dynamic_slice_in_dim(grads, core * half, half, 0)
    theirs = lax.dynamic_slice_in_dim(grads, (1 - core) * half, half, 0)
    total = mine + swapped(theirs, "group", n_group, 1)
    share = half // 2
    kept = lax.dynamic_slice_in_dim(total, side * share, share, 0)
    other = lax.dynamic_slice_in_dim(total, (1 - side) * share, share, 0)
    got = [swapped(other if k % 2 else kept, "group", n_group, 2 * k) for k in range(1, n_group // 2)]
    for piece in got:
        kept = kept + piece
    means = [lax.dynamic_index_in_dim(mean_tiles, band, 0, keepdims=False)]
    arrived = []
    for k in range(1, n_band):
        target = lax.rem(band + k, n_band)
        sent = jnp.concatenate([kept, lax.dynamic_index_in_dim(mean_tiles, target, 0, keepdims=False)])
        arrived.append(shifted(sent, "band", n_band, k))
    for piece in arrived:
        kept = kept + piece[:share]
        means.append(piece[share:])
    other = swapped(kept, "group", n_group, 2)
    whole = jnp.where(side == 0, jnp.concatenate([kept, other]), jnp.concatenate([other, kept]))
    return whole, swapped(whole, "group", n_group, 1), means


def vmem(*shape, dtype=BF16):
    return pltpu.VMEM(shape, dtype)


def local(
    station_rows,
    station_lons,
    station_obs,
    station_live,
    block_band,
    truth_field,
    length_scales,
    w_in,
    w_down,
    w_mid,
    w_up,
    w_head,
):
    n_band = lax.axis_size("band")
    n_group = lax.axis_size("group")
    n_blocks = station_rows.shape[1]
    lon_count = truth_field.shape[2]
    own_tiles = -(-(-(-lon_count // LANES)) // n_band)
    own = own_tiles * LANES
    window = own + 2 * HALO
    half = window // 2
    rows = ROWS_BAND * n_band
    coarse = rows // 2
    hist_tiles = (window + 2 * REACH) // LANES

    sizes = (n_band, n_blocks, own, lon_count)
    pay_rows = 3 * n_blocks + 8 + -(-(window // LANES) * ROWS_BAND // 8) * 8
    wide_lanes = (n_band * own_tiles + 1) * LANES
    in_vmem = pl.BlockSpec(memory_space=pltpu.VMEM)
    in_hbm = pl.BlockSpec(memory_space=pltpu.HBM)

    def in_place(arg):
        return pltpu.with_memory_space_constraint(arg, pltpu.HBM)

    def shaped(*shape, dtype=BF16):
        return jax.ShapeDtypeStruct(shape, dtype)

    arrays = (
        station_rows, station_lons, station_obs, station_live, block_band.reshape(1, n_blocks), truth_field,
        length_scales.reshape(1, 4),
    )
    packed = pl.pallas_call(
        functools.partial(pack_kernel, sizes),
        out_shape=(shaped(pay_rows, LANES, dtype=F32),) * n_band,
        in_specs=[in_hbm] * 7,
        out_specs=(in_vmem,) * n_band,
        scratch_shapes=[vmem(ROWS_BAND, wide_lanes, dtype=F32)]
        + [vmem(*arg.shape, dtype=arg.dtype) for arg in arrays]
        + [pltpu.SemaphoreType.DMA((7,))],
        compiler_params=pltpu.CompilerParams(vmem_limit_bytes=8 * 1024 * 1024),
    )(*[in_place(arg) for arg in arrays])
    pays = [packed[0]] + [swapped(packed[k], "band", n_band, k) for k in range(1, n_band)]

    hist_shape = (n_band, hist_tiles * 32, LANES)
    weights = (jnp.transpose(w_in, (0, 1, 3, 2)), w_down, w_mid, w_up, w_head)
    early = pl.pallas_call(
        functools.partial(early_kernel, sizes),
        out_shape=(
            shaped(*hist_shape, dtype=F32),
            shaped(4, 4 * LANES, 2 * LANES),
            shaped(256, 192),
            shaped(64, 768),
            shaped(128, 576),
            shaped(128, 1024),
            shaped(16, 256),
            shaped(256, 16),
            shaped(256, 512),
            shaped(128, 576),
            shaped(256, 384),
        ),
        in_specs=[in_vmem] + [in_hbm] * 5,
        out_specs=(in_vmem,) * 11,
        scratch_shapes=[
            pltpu.SMEM((8, LANES), F32),
            vmem(n_blocks, LANES, dtype=F32),
            vmem(n_blocks, LANES, dtype=F32),
            vmem(256, 256, dtype=F32),
            vmem(32, 512, dtype=F32),
            vmem(128, 576, dtype=F32),
            vmem(64, 768, dtype=F32),
            vmem(384, 128, dtype=F32),
            vmem(640, 128, dtype=F32),
            vmem(384, 256, dtype=F32),
        ]
        + [vmem(*arg.shape) for arg in weights]
        + [pltpu.SemaphoreType.DMA((6,))],
        compiler_params=pltpu.CompilerParams(vmem_limit_bytes=16 * 1024 * 1024),
        cost_estimate=pl.CostEstimate(flops=200_000_000, bytes_accessed=2_000_000, transcendentals=700_000),
    )(packed[0], *[in_place(arg) for arg in weights])

    _, grads, mean_tiles = pl.pallas_call(
        functools.partial(network_kernel, sizes),
        out_shape=(
            shaped(*hist_shape, dtype=F32),
            shaped(384, LANES, dtype=F32),
            shaped(n_band, own_tiles, ROWS_BAND, LANES, dtype=F32),
        ),
        in_specs=[in_vmem] * (n_band + 11),
        out_specs=(in_vmem, in_vmem, in_vmem),
        input_output_aliases={n_band: 0},
        scratch_shapes=[
            pltpu.SMEM((n_band, 8, LANES), F32),
            pltpu.SemaphoreType.DMA((n_band,)),
            vmem(rows + 2, 32, half),
            vmem(rows, 64, half, dtype=F32),
            vmem(rows + 2, 256, half),
            vmem(coarse, 32, half, dtype=F32),
            vmem(2, coarse // 2 + 2, 96, half),
            vmem(coarse, 32, half, dtype=F32),
            vmem(rows, 64, half, dtype=F32),
            vmem(rows, 64, half),
            vmem(n_band, 8, half, dtype=F32),
            vmem(n_band, 16, 2 * half),
            vmem(rows + 2, 128, half),
            vmem(rows + 2, 64, half),
            vmem(rows, 64, half),
            vmem(2, coarse // 2 + 2, 32, half),
            vmem(2, coarse // 2 + 2, 96, half),
            vmem(coarse + 2, 32, half),
            vmem(coarse + 2, 96, half),
            vmem(rows + 2, 64, half),
            vmem(n_band, n_blocks, LANES, dtype=F32),
            vmem(n_band, n_blocks, LANES, dtype=F32),
            vmem(192, 256, dtype=F32),
            vmem(96, 256, dtype=F32),
            vmem(96, 96, dtype=F32),
            vmem(32, 192, dtype=F32),
            vmem(16, 256, dtype=F32),
        ],
        compiler_params=pltpu.CompilerParams(vmem_limit_bytes=40 * 1024 * 1024),
        cost_estimate=pl.CostEstimate(flops=4_000_000_000, bytes_accessed=4_000_000, transcendentals=2_000_000),
    )(*pays, *early)

    low, high, means = reduced(grads, mean_tiles.reshape(n_band, own_tiles * ROWS_BAND, LANES), n_band, n_group)
    means = [piece.reshape(own_tiles, ROWS_BAND, LANES) for piece in means]
    outs = pl.pallas_call(
        functools.partial(unpack_kernel, (n_band, own, lon_count)),
        out_shape=(
            jax.ShapeDtypeStruct((1, ROWS_BAND, lon_count), F32),
            jax.ShapeDtypeStruct((3, 3, 8, 32), F32),
            jax.ShapeDtypeStruct((4, 4, 32, 32), F32),
            jax.ShapeDtypeStruct((3, 3, 32, 32), F32),
            jax.ShapeDtypeStruct((3, 3, 32, 64), F32),
            jax.ShapeDtypeStruct((2, 32), F32),
        ),
        in_specs=[in_vmem] * (2 + n_band),
        out_specs=(in_vmem,) * 6,
        scratch_shapes=[vmem(ROWS_BAND, n_band * own, dtype=F32)],
        compiler_params=pltpu.CompilerParams(vmem_limit_bytes=16 * 1024 * 1024),
    )(low, high, *means)
    return (outs[0], jnp.transpose(outs[1], (0, 1, 3, 2))) + tuple(outs[2:])


def solution(mesh):
    return jax.shard_map(
        local,
        mesh=mesh,
        in_specs=(
            P("group", "band", None),
            P("group", "band", None),
            P("group", "band", None),
            P("group", "band", None),
            P("group", "band", None),
            P("group", "band", None),
            P(),
            P(),
            P(),
            P(),
            P(),
            P(),
        ),
        out_specs=(P("group", "band", None), P(), P(), P(), P(), P()),
        check_vma=False,
    )
```

```python
import functools

import jax
import jax.numpy as jnp
from jax import lax
from jax.experimental import pallas as pl
from jax.experimental.pallas import tpu as pltpu
from jax.sharding import PartitionSpec as P

LANES = 128
HALO = 64
REACH = 128
ROWS_BAND = 4
FAR = -1.0e6
F32 = jnp.float32
BF16 = jnp.bfloat16


def looped(count, step, body):
    step = min(step, count)
    if count == step:
        for index in range(count):
            body(index)
    else:

        def turn(outer, carry):
            for inner in range(step):
                body(outer * step + inner)
            return carry

        lax.fori_loop(0, count // step, turn, 0)


def dot(first, second):
    return jnp.dot(first, second, preferred_element_type=F32)


def dot_lanes(first, second):
    return lax.dot_general(first, second, (((1,), (1,)), ((), ())), preferred_element_type=F32)


def iota(shape, dim):
    return lax.broadcasted_iota(jnp.int32, shape, dim)


def rolled(values, shift):
    width = values.shape[-1]
    return pltpu.roll(values, shift % width, values.ndim - 1)


def four_shifts(even, odd):
    return jnp.concatenate([rolled(odd, 1), even, odd, rolled(even, -1)], axis=0)


def three_shifts(values, width):
    return jnp.concatenate([rolled(values, width), values, rolled(values, -width)], axis=0)


def sigmoid(values):
    return 0.5 + 0.5 * jnp.tanh(0.5 * values)


def silu_and_slope(values):
    squash = sigmoid(values)
    hidden = values * squash
    return hidden, squash + hidden * (1.0 - squash)


def split_three(values):
    high = values.astype(BF16).astype(F32)
    rest = values - high
    middle = rest.astype(BF16).astype(F32)
    return high, middle, rest - middle


def station_sums(own, lon_count, n_blocks, step, me, pay, bands, scales, hist, hi_pos, lo_pos):
    hist_tiles = hist.shape[1] // 32
    start = (me * own - HALO - REACH).astype(F32)
    place = pay[n_blocks : 2 * n_blocks] - start
    place = jnp.where(place < 0.0, place + lon_count, place)
    place = jnp.where(place < 0.0, place + lon_count, place)
    place = jnp.where(place >= lon_count, place - lon_count, place)
    tile_of = jnp.floor(place * (1.0 / LANES))
    hi_pos[...] = tile_of
    lo_pos[...] = place - tile_of * LANES

    m_index = iota((32, 1), 0)
    row_of = ((m_index % 8) // 2).astype(F32)
    scale_of = m_index // 8
    kind_of = m_index % 2
    spread = jnp.where(
        scale_of == 0, scales[0], jnp.where(scale_of == 1, scales[1], jnp.where(scale_of == 2, scales[2], scales[3]))
    )
    rate = -0.5 / (spread * spread)
    lane_iota = iota((LANES, LANES), 0).astype(F32)

    def one_block(block):
        at_row = pay[pl.ds(block, 1), :]
        observed = pay[pl.ds(2 * n_blocks + block, 1), :]
        high = hi_pos[pl.ds(block, 1), :]
        low = lo_pos[pl.ds(block, 1), :]
        gap = row_of - at_row
        left = jnp.exp(gap * gap * rate) * jnp.where(kind_of == 0, 1.0, observed)
        spread_left = jnp.concatenate(
            [jnp.where(high == float(tile), left, 0.0) for tile in range(hist_tiles)], axis=0
        ).astype(BF16)
        one_hot = jnp.where(lane_iota == low, 1.0, 0.0).astype(BF16)
        band = bands[0, block].astype(jnp.int32)
        hist[band] = hist[band] + dot_lanes(spread_left, one_hot)

    looped(n_blocks, step, one_block)


def pack_kernel(sizes, *refs):
    n_band, n_blocks, own, lon_count = sizes
    pays = refs[7 : 7 + n_band]
    wide = refs[7 + n_band]
    held, sems = refs[8 + n_band : 15 + n_band], refs[15 + n_band]
    copies = [pltpu.make_async_copy(refs[k], held[k], sems.at[k]) for k in range(7)]
    for copy in copies:
        copy.start()
    for copy in copies:
        copy.wait()
    rows, lons, obs, live, block_band, field, scales = held
    me = lax.axis_index("band")
    at_row = rows[0].astype(F32)
    lon = jnp.where(live[0] > 0, lons[0].astype(F32), FAR)
    total = wide.shape[1]
    wide[:, 0:HALO] = field[0, :, lon_count - HALO : lon_count]
    wide[:, HALO : HALO + lon_count] = field[0]
    wide[:, HALO + lon_count : total] = field[0, :, 0 : total - HALO - lon_count]
    for shift in range(n_band):
        pay = pays[shift]
        pay[0:n_blocks] = at_row
        pay[n_blocks : 2 * n_blocks] = lon
        pay[2 * n_blocks : 3 * n_blocks] = obs[0]
        pay[3 * n_blocks : 3 * n_blocks + 8] = jnp.zeros((8, LANES), F32)
        pay[3 * n_blocks : 3 * n_blocks + 1, 0:n_blocks] = block_band[...].astype(F32)
        pay[3 * n_blocks + 1 : 3 * n_blocks + 2, 0:4] = scales[...]
        target = me ^ shift
        for tile in range((own + 2 * HALO) // LANES):
            at = pl.multiple_of(target * own + tile * LANES, LANES)
            first = 3 * n_blocks + 8 + ROWS_BAND * tile
            pay[first : first + ROWS_BAND] = wide[:, pl.ds(at, LANES)]


def early_kernel(sizes, *refs):
    n_band, n_blocks, own, lon_count = sizes
    pay, w_in, w_head = refs[:3]
    hist, table, w1, wd, wm, wu, wh, wht, wf, wmf, wbd = refs[6:17]
    bands, hi_pos, lo_pos, t1, td, tm, tu, tf, tmf, tbd = refs[17:27]
    held, sems = refs[27:30], refs[30]
    me = lax.axis_index("band")
    band_copy = pltpu.make_async_copy(pay.at[pl.ds(3 * n_blocks, 8)], bands, sems.at[3])
    band_copy.start()
    copies = [pltpu.make_async_copy(refs[3 + k], held[k], sems.at[k]) for k in range(3)]
    for copy in copies:
        copy.start()
    place_in = iota((4 * LANES, 2 * LANES), 0)
    place_out = iota((4 * LANES, 2 * LANES), 1)
    distance = (place_in - (REACH + 2 * (place_out % LANES) + place_out // LANES)).astype(F32)
    squared = distance * distance
    band_copy.wait()
    scales = [bands[1, k] for k in range(4)]
    hist[...] = jnp.zeros_like(hist)
    step = n_blocks if n_band <= 4 else 4
    station_sums(own, lon_count, n_blocks, step, me, pay, bands, scales, hist, hi_pos, lo_pos)
    for scale in range(4):
        table[scale] = jnp.exp(squared * (-0.5 / (scales[scale] * scales[scale]))).astype(BF16)

    for copy in copies:
        copy.wait()
    w_down, w_mid, w_up = held
    for held in (t1, tm, tu, tf, tmf, tbd):
        held[...] = jnp.zeros_like(held)
    for row in range(3):
        for col in range(3):
            inner = w_in[row, col].astype(F32)
            mid = w_mid[row, col].astype(F32)
            up = w_up[row, col].astype(F32)
            back = (2 - row) * 3 + 2 - col
            for out in range(4):
                at = out * 96 + (row * 3 + col) * 32
                tm[out * 32 : out * 32 + 32, at : at + 32] = mid
                at = out * 96 + back * 32
                tmf[at : at + 32, out * 32 : out * 32 + 32] = mid
            for phase in range(2):
                for out in range(4):
                    at = (out + row) * 32 + (phase + col) * 8
                    to = out * 64 + phase * 32
                    t1[at : at + 8, to : to + 32] = inner
                for part in range(2):
                    cols = slice(part * 32, part * 32 + 32)
                    at = (row * 2 + part) * 128 + (phase + col) * 32
                    tu[phase * 32 : phase * 32 + 32, at : at + 32] = up[:, cols]
                    at = (2 - row) * 128 + (phase + 2 - col) * 32
                    to = part * 64 + phase * 32
                    tf[at : at + 32, to : to + 32] = up[:, cols]
    sides = (((1, 0), (3, -1)), ((0, 1), (2, 0)))
    for row in range(4):
        for col in range(4):
            td[:, (row * 4 + col) * 32 : (row * 4 + col) * 32 + 32] = w_down[row, col].astype(F32)
    for side in range(2):
        for phase in range(2):
            for row, row_shift in sides[side]:
                for col, col_shift in sides[phase]:
                    for out in range(2):
                        at = (out + row_shift + 1) * 96 + (col_shift + 1) * 32
                        to = out * 128 + (side * 2 + phase) * 32
                        tbd[at : at + 32, to : to + 32] = w_down[row, col].astype(F32)

    def two_rows(one, shift):
        empty = jnp.zeros((one.shape[0], shift), F32)
        return jnp.concatenate(
            [jnp.concatenate([one, empty], axis=1), jnp.concatenate([empty, one], axis=1)], axis=0
        ).astype(BF16)

    w1[...] = t1[...].T[:, 0:192].astype(BF16)
    wd[...] = two_rows(td[...], 256)
    wm[...] = tm[...].astype(BF16)
    wu[...] = two_rows(tu[...], 256)
    wf[...] = two_rows(tf[...].T, 128)
    wmf[...] = tmf[...].T[:, 0:576].astype(BF16)
    wbd[...] = tbd[...].T.astype(BF16)
    heads = w_head[...].astype(F32)
    heads = jnp.concatenate([heads, jnp.zeros((6, 32), F32)], axis=0)
    heads = jnp.concatenate([heads, jnp.zeros((8, 96), F32)], axis=1)
    heads = heads + rolled(heads, 32)
    heads = heads + rolled(heads, 64)
    heads = jnp.concatenate([heads, heads], axis=1)
    k_index = iota((128, 256), 0)
    c_index = iota((128, 256), 1) // 32
    same = (k_index % 4 == c_index // 2) & ((k_index // 4) % 2 == c_index % 2) & (k_index < 16)
    full = jnp.where(same, jnp.where(k_index < 8, heads[0:1], heads[1:2]), 0.0)
    wh[...] = full[0:16].astype(BF16)
    wht[...] = full.T[:, 0:16].astype(BF16)


def network_kernel(sizes, *refs):
    n_band, n_blocks, own, lon_count = sizes
    window = own + 2 * HALO
    half = window // 2
    rows = ROWS_BAND * n_band
    coarse = rows // 2
    own_tiles = own // LANES
    pays = refs[:n_band]
    (hist_own, table, w1, wd, wm, wu, wh, wht, wf, wmf, wbd) = refs[n_band : n_band + 11]
    hist, grads_out, mean_out = refs[n_band + 11 : n_band + 14]
    (
        bands, band_sems, zf, p1, zj, p2, z2, p3, p4, h4, truth, mean_split,
        gs, gp4m, gj, gp3m, zg3, gp2m, zg2, gp1m, hi_pos, lo_pos,
        acc_up, acc_down, acc_mid, acc_in, acc_head,
    ) = refs[n_band + 14 :]
    many = n_band > 4
    me = lax.axis_index("band")
    cell_count = float(rows * lon_count)

    copies = [
        pltpu.make_async_copy(pays[k].at[pl.ds(3 * n_blocks, 8)], bands.at[k], band_sems.at[k])
        for k in range(1, n_band)
    ]
    for copy in copies:
        copy.start()
    for edge in (0, rows + 1):
        zf[edge] = jnp.zeros((32, half), BF16)
        zj[edge] = jnp.zeros((256, half), BF16)
        gs[edge] = jnp.zeros((128, half), BF16)
        gp4m[edge] = jnp.zeros((64, half), BF16)
        gp1m[edge] = jnp.zeros((64, half), BF16)
    for edge in (0, coarse + 1):
        zg2[edge] = jnp.zeros((96, half), BF16)
        gp2m[edge] = jnp.zeros((32, half), BF16)
    for edge in (0, coarse // 2 + 1):
        for par in range(2):
            z2[par, edge] = jnp.zeros((96, half), BF16)
            zg3[par, edge] = jnp.zeros((96, half), BF16)
            gp3m[par, edge] = jnp.zeros((32, half), BF16)
    fine_iota = iota((2 * LANES, 2 * LANES), 0)
    part_iota = iota((2 * LANES, 2 * LANES), 1)
    parting = (fine_iota == 2 * (part_iota % LANES) + part_iota // LANES).astype(F32).astype(BF16)
    chunks = window // (2 * LANES)
    for source in range(n_band):
        at = me ^ source
        pieces = []
        for chunk in range(2):
            if chunk < chunks:
                tiles = [
                    pays[source][
                        3 * n_blocks + 8 + (2 * chunk + t) * ROWS_BAND : 3 * n_blocks + 8 + (2 * chunk + t + 1) * ROWS_BAND
                    ]
                    for t in range(2)
                ]
                pieces.append(jnp.concatenate(tiles, axis=1))
            else:
                pieces.append(jnp.zeros((ROWS_BAND, 2 * LANES), F32))
        stacked = jnp.concatenate(split_three(jnp.concatenate(pieces, axis=0)) + (jnp.zeros((8, 2 * LANES), F32),), axis=0)
        parted = dot(stacked.astype(BF16), parting)
        parted = parted[0:8] + parted[8:16] + parted[16:24]
        for chunk in range(chunks):
            for phase in range(2):
                truth[at, phase * 4 : phase * 4 + 4, chunk * LANES : (chunk + 1) * LANES] = parted[
                    chunk * 4 : chunk * 4 + 4, phase * LANES : (phase + 1) * LANES
                ]

    for copy in copies:
        copy.wait()
    scales = [bands[1, 1, k] for k in range(4)]
    for source in range(1, n_band):
        station_sums(
            own, lon_count, n_blocks, 4 if many else n_blocks, me, pays[source], bands.at[source], scales,
            hist, hi_pos.at[source], lo_pos.at[source],
        )

    eight = 8 * n_band
    chunks = half // LANES
    sub = iota((8, 1), 0)
    per_scale = []
    for scale in range(4):
        stacked = []
        for chunk in range(chunks):
            tiles = [
                hist[:, (2 * chunk + t) * 32 + 8 * scale : (2 * chunk + t) * 32 + 8 * scale + 8, :].reshape(eight, LANES)
                for t in range(4)
            ]
            stacked.append(jnp.concatenate(tiles, axis=1))
        cells = jnp.concatenate(stacked, axis=0)
        high = cells.astype(BF16)
        low = (cells - high.astype(F32)).astype(BF16)
        both = dot(jnp.concatenate([high, low], axis=0), table[scale])
        total = both[: chunks * eight] + both[chunks * eight :]
        below = pltpu.roll(total, 1, 0)
        density = jnp.where(iota((chunks * eight, 1), 0) % 2 == 0, total, below)
        per_scale.append(total / (1.0 + density))

    def phase_rows(phase):
        lines = []
        for band in range(n_band):
            parts = [
                jnp.concatenate(
                    [
                        per_scale[scale][
                            chunk * eight + 8 * band : chunk * eight + 8 * band + 8,
                            phase * LANES : (phase + 1) * LANES,
                        ]
                        for chunk in range(chunks)
                    ],
                    axis=1,
                )
                for scale in range(4)
            ]
            for row in range(ROWS_BAND):
                line = None
                for scale in range(4):
                    turn = (2 * scale - 2 * row) % 8
                    moved = pltpu.roll(parts[scale], turn, 0) if turn else parts[scale]
                    line = moved if line is None else jnp.where(sub // 2 == scale, moved, line)
                lines.append(line)
        return jnp.concatenate(lines, axis=0)

    even, odd = phase_rows(0), phase_rows(1)
    odd_before = rolled(odd, 1)
    even_after = rolled(even, -1)
    for row in range(rows):
        pick = slice(row * 8, row * 8 + 8)
        zf[row + 1] = jnp.concatenate(
            [odd_before[pick], even[pick], odd[pick], even_after[pick]], axis=0
        ).astype(BF16)

    def first(group):
        pre = dot(w1[...], zf[pl.ds(4 * group, 6)].reshape(192, half))
        for out in range(4):
            row = 4 * group + out
            hidden, p1[row] = silu_and_slope(pre[64 * out : 64 * out + 64])
            zj[row + 1, 128:256, :] = four_shifts(hidden[:32], hidden[32:]).astype(BF16)

    looped(n_band, 1 if many else n_band, first)

    def second(index):
        pre = dot(wd[...], zj[pl.ds(4 * index, 6), 128:256, :].reshape(768, half))
        for par in range(2):
            row = 2 * index + par
            hidden, p2[row] = silu_and_slope(pre[32 * par : 32 * par + 32])
            z2[par, index + 1] = three_shifts(hidden, 2).astype(BF16)

    looped(coarse // 2, 4 if many else coarse // 2, second)

    def third(group):
        for par in range(2):
            pre = dot(wm[...], z2[par, pl.ds(4 * group, 6)].reshape(576, half))
            for out in range(4):
                row = 2 * (4 * group + out) + par
                hidden, p3[row] = silu_and_slope(pre[32 * out : 32 * out + 32])
                wide = four_shifts(hidden, hidden).astype(BF16)
                zj[2 * row + 1, 0:128, :] = wide
                zj[2 * row + 2, 0:128, :] = wide

    looped(coarse // 8, 1, third)

    def fourth(pair):
        pre = dot(wu[...], zj[pl.ds(2 * pair, 4)].reshape(1024, half))
        for out in range(2):
            row = 2 * pair + out
            hidden, p4[row] = silu_and_slope(pre[64 * out : 64 * out + 64])
            h4[row] = hidden.astype(BF16)

    looped(rows // 2, 2 if many else rows // 2, fourth)

    own_cells = jnp.clip(lon_count - me * own, 0, own) // 2
    place = iota((1, half), 1)
    mask = ((place >= HALO // 2) & (place < HALO // 2 + own_cells)).astype(F32)
    acc_head[...] = jnp.zeros_like(acc_head)

    def head(group):
        hidden = h4[pl.ds(4 * group, 4)].reshape(256, half)
        out = dot(wh[...], hidden)
        mean = out[:8]
        raw = out[8:]
        decay = jnp.exp(-jnp.abs(raw))
        noise = 0.1 + (jnp.maximum(raw, 0.0) + jnp.log1p(decay))
        error = (mean - truth[group]) / noise
        weight = 1.0 / (noise * cell_count)
        grad_mean = error * weight
        grad_raw = (1.0 - error * error) * weight * sigmoid(raw)
        grad_out = jnp.concatenate([grad_mean, grad_raw], axis=0)
        grad_bf = grad_out.astype(BF16)
        acc_head[...] += dot_lanes((grad_out * mask).astype(BF16), hidden)
        back = dot(wht[...], grad_bf)
        grad = back * p4[pl.ds(4 * group, 4)].reshape(256, half)
        for row in range(4):
            mine = grad[row * 64 : row * 64 + 64]
            gp4m[4 * group + row + 1] = (mine * mask).astype(BF16)
            gs[4 * group + row + 1] = four_shifts(mine[:32], mine[32:]).astype(BF16)
        parts = split_three(jnp.concatenate([mean[0:4], mean[4:8]], axis=1))
        mean_split[group] = jnp.concatenate(
            parts + (jnp.zeros((4, 2 * half), F32),), axis=0
        ).astype(BF16)

    looped(n_band, 1 if many else n_band, head)

    target = iota((2 * half, own), 1) + HALO
    origin = iota((2 * half, own), 0)
    joining = (target == 2 * (origin % half) + origin // half).astype(F32).astype(BF16)
    joined = dot(mean_split[...].reshape(16 * n_band, 2 * half), joining)
    for band in range(n_band):
        four = joined[16 * band : 16 * band + 8] + joined[16 * band + 8 : 16 * band + 16]
        four = four[0:4] + four[4:8]
        for tile in range(own_tiles):
            mean_out[band, tile] = four[:, tile * LANES : (tile + 1) * LANES]

    acc_up[...] = jnp.zeros_like(acc_up)
    acc_down[...] = jnp.zeros_like(acc_down)
    acc_mid[...] = jnp.zeros_like(acc_mid)
    acc_in[...] = jnp.zeros_like(acc_in)

    def join_back(index):
        for par in range(2):
            row = 2 * index + par
            back = dot(wf[...], gs[pl.ds(2 * row, 4)].reshape(512, half)).astype(BF16)
            total = None
            for side in range(2):
                mine = back[128 * side : 128 * side + 128]
                gj[2 * row + side] = mine[64:]
                up = mine[:64].astype(F32)
                part = up[:32] + up[32:]
                total = part if total is None else total + part
            grad = total * p3[row]
            gp3m[par, index + 1] = (grad * mask).astype(BF16)
            zg3[par, index + 1] = three_shifts(grad, 2).astype(BF16)

    looped(coarse // 2, 2 if many else coarse // 2, join_back)

    def weights_up(row):
        acc_up[...] += dot_lanes(gp4m[pl.ds(row, 3)].reshape(192, half), zj[row + 1])

    looped(rows, 4 if many else rows, weights_up)

    def mid_back(group):
        for par in range(2):
            back = dot(wmf[...], zg3[par, pl.ds(4 * group, 6)].reshape(576, half))
            for out in range(4):
                row = 2 * (4 * group + out) + par
                grad = back[32 * out : 32 * out + 32] * p2[row]
                gp2m[row + 1] = (grad * mask).astype(BF16)
                zg2[row + 1] = three_shifts(grad, 1).astype(BF16)

    looped(coarse // 8, 1, mid_back)

    def weights_mid(index):
        for par in range(2):
            acc_mid[...] += dot_lanes(gp3m[par, pl.ds(index, 3)].reshape(96, half), z2[par, index + 1])

    looped(coarse // 2, 4 if many else coarse // 2, weights_mid)

    def down_back(pair):
        back = dot(wbd[...], zg2[pl.ds(2 * pair, 4)].reshape(384, half))
        for out in range(4):
            fine = 4 * pair + out
            grad = (back[64 * out : 64 * out + 64] + gj[fine].astype(F32)) * p1[fine]
            gp1m[fine + 1] = (grad * mask).astype(BF16)

    looped(coarse // 2, 2 if many else coarse // 2, down_back)

    def weights_down(row):
        acc_down[...] += dot_lanes(
            gp2m[pl.ds(row, 3)].reshape(96, half),
            zj[pl.ds(2 * row + 1, 2), 128:256, :].reshape(256, half),
        )

    looped(coarse, 4 if many else coarse, weights_down)

    def weights_in(row):
        acc_in[...] += dot_lanes(zf[row + 1], gp1m[pl.ds(row, 3)].reshape(192, half))

    looped(rows, 4 if many else rows, weights_in)

    up = acc_up[...]
    for step in range(3):
        first_up, second_up = up[64 * step : 64 * step + 32], up[64 * step + 32 : 64 * step + 64]
        for part in range(2):
            cols = slice(128 * part, 128 * part + 128)
            grads_out[96 * part + 32 * step : 96 * part + 32 * step + 32, :] = first_up[:, cols] + rolled(
                second_up[:, cols], -32
            )
    mid = acc_mid[...]
    grads_out[0:96, 96:128] = mid[:, 0:32]
    grads_out[96:192, 96:128] = mid[:, 32:64]
    down = acc_down[...]
    for tap, (step, side) in enumerate(((2, 1), (1, 0), (1, 1), (0, 0))):
        grads_out[192 + 32 * tap : 224 + 32 * tap, :] = down[
            32 * step : 32 * step + 32, 128 * side : 128 * side + 128
        ]
    inner = acc_in[...]
    for step in range(3):
        grads_out[320:344, 32 * step : 32 * step + 32] = (
            inner[0:24, 64 * step : 64 * step + 32] + inner[8:32, 64 * step + 32 : 64 * step + 64]
        )
    for part in range(4):
        grads_out[344:368, 32 * part : 32 * part + 32] = mid[24 * part : 24 * part + 24, 64:96]
    grads_out[320:344, 96:128] = jnp.zeros((24, 32), F32)
    grads_out[368:384] = jnp.zeros((16, LANES), F32)
    k_index = iota((16, 256), 0) % 8
    c_index = iota((16, 256), 1) // 32
    same = (k_index % 4 == c_index // 2) & (k_index // 4 == c_index % 2)
    heads = jnp.where(same, acc_head[...], 0.0)
    for kind in range(2):
        line = jnp.sum(heads[8 * kind : 8 * kind + 8], axis=0, keepdims=True)
        line = line[:, :128] + line[:, 128:]
        line = line + rolled(line, 64)
        line = line + rolled(line, 32)
        grads_out[320 + kind : 321 + kind, 96:128] = line[:, 96:128]


def unpack_kernel(sizes, *refs):
    n_band, own, lon_count = sizes
    low, high = refs[0], refs[1]
    means = refs[2 : 2 + n_band]
    mean_out, grad_in, grad_down, grad_mid, grad_up, grad_head, wide = refs[2 + n_band :]
    me = lax.axis_index("band")
    core = lax.rem(lax.axis_index("group"), 2)
    own_tiles = own // LANES
    first = jnp.where(core == 0, low[...], high[...])
    second = jnp.where(core == 0, high[...], low[...])
    part_a, part_b = first[0:96], first[96:192]
    down, inner, folded = second[0:128], second[128:152], second[152:176]
    last = jnp.concatenate([rolled(folded, -32 * part) for part in range(4)], axis=0)
    lane = iota((96, LANES), 1)
    mids = (rolled(part_a, -96), rolled(part_b, -96), last)
    for tap_col in range(3):
        ups = jnp.where(lane < 32, rolled(part_a, -32 * tap_col), rolled(part_b, 32 - 32 * tap_col))
        for tap_row in range(3):
            at = slice(32 * (2 - tap_row), 32 * (2 - tap_row) + 32)
            grad_up[tap_row, tap_col] = ups[at, 0:64]
            grad_mid[tap_row, tap_col] = mids[tap_col][at, 0:32]
    for tap_row in range(3):
        ins = rolled(inner, -32 * (2 - tap_row))
        for tap_col in range(3):
            grad_in[tap_row, tap_col] = ins[8 * tap_col : 8 * tap_col + 8, 0:32]
    for tap_col in range(4):
        downs = rolled(down, -32 * tap_col)
        for tap_row in range(4):
            grad_down[tap_row, tap_col] = downs[32 * tap_row : 32 * tap_row + 32, 0:32]
    grad_head[...] = rolled(inner[0:8], -96)[0:2, 0:32]
    for shift in range(n_band):
        origin = lax.rem(me - shift + n_band, n_band)
        for tile in range(own_tiles):
            at = pl.multiple_of((origin * own_tiles + tile) * LANES, LANES)
            wide[:, pl.ds(at, LANES)] = means[shift][tile]
    mean_out[0] = wide[:, 0:lon_count]


def swapped(values, axis, count, bits):
    return lax.ppermute(values, axis, [(i, i ^ bits) for i in range(count)])


def shifted(values, axis, count, shift):
    return lax.ppermute(values, axis, [(i, (i + shift) % count) for i in range(count)])


def reduced(grads, mean_tiles, n_band, n_group):
    group = lax.axis_index("group")
    band = lax.axis_index("band")
    core, side = group % 2, (group // 2) % 2
    half = grads.shape[0] // 2
    mine = lax.dynamic_slice_in_dim(grads, core * half, half, 0)
    theirs = lax.dynamic_slice_in_dim(grads, (1 - core) * half, half, 0)
    total = mine + swapped(theirs, "group", n_group, 1)
    share = half // 2
    kept = lax.dynamic_slice_in_dim(total, side * share, share, 0)
    other = lax.dynamic_slice_in_dim(total, (1 - side) * share, share, 0)
    got = [swapped(other if k % 2 else kept, "group", n_group, 2 * k) for k in range(1, n_group // 2)]
    for piece in got:
        kept = kept + piece
    means = [lax.dynamic_index_in_dim(mean_tiles, band, 0, keepdims=False)]
    arrived = []
    for k in range(1, n_band):
        target = lax.rem(band + k, n_band)
        sent = jnp.concatenate([kept, lax.dynamic_index_in_dim(mean_tiles, target, 0, keepdims=False)])
        arrived.append(shifted(sent, "band", n_band, k))
    for piece in arrived:
        kept = kept + piece[:share]
        means.append(piece[share:])
    other = swapped(kept, "group", n_group, 2)
    whole = jnp.where(side == 0, jnp.concatenate([kept, other]), jnp.concatenate([other, kept]))
    return whole, swapped(whole, "group", n_group, 1), means


def vmem(*shape, dtype=BF16):
    return pltpu.VMEM(shape, dtype)


def local(
    station_rows,
    station_lons,
    station_obs,
    station_live,
    block_band,
    truth_field,
    length_scales,
    w_in,
    w_down,
    w_mid,
    w_up,
    w_head,
):
    n_band = lax.axis_size("band")
    n_group = lax.axis_size("group")
    n_blocks = station_rows.shape[1]
    lon_count = truth_field.shape[2]
    own_tiles = -(-(-(-lon_count // LANES)) // n_band)
    own = own_tiles * LANES
    window = own + 2 * HALO
    half = window // 2
    rows = ROWS_BAND * n_band
    coarse = rows // 2
    hist_tiles = (window + 2 * REACH) // LANES

    sizes = (n_band, n_blocks, own, lon_count)
    pay_rows = 3 * n_blocks + 8 + -(-(window // LANES) * ROWS_BAND // 8) * 8
    wide_lanes = (n_band * own_tiles + 1) * LANES
    in_vmem = pl.BlockSpec(memory_space=pltpu.VMEM)
    in_hbm = pl.BlockSpec(memory_space=pltpu.HBM)

    def in_place(arg):
        return pltpu.with_memory_space_constraint(arg, pltpu.HBM)

    def shaped(*shape, dtype=BF16):
        return jax.ShapeDtypeStruct(shape, dtype)

    arrays = (
        station_rows, station_lons, station_obs, station_live, block_band.reshape(1, n_blocks), truth_field,
        length_scales.reshape(1, 4),
    )
    packed = pl.pallas_call(
        functools.partial(pack_kernel, sizes),
        out_shape=(shaped(pay_rows, LANES, dtype=F32),) * n_band,
        in_specs=[in_hbm] * 7,
        out_specs=(in_vmem,) * n_band,
        scratch_shapes=[vmem(ROWS_BAND, wide_lanes, dtype=F32)]
        + [vmem(*arg.shape, dtype=arg.dtype) for arg in arrays]
        + [pltpu.SemaphoreType.DMA((7,))],
        compiler_params=pltpu.CompilerParams(vmem_limit_bytes=8 * 1024 * 1024),
    )(*[in_place(arg) for arg in arrays])
    pays = [packed[0]] + [swapped(packed[k], "band", n_band, k) for k in range(1, n_band)]

    hist_shape = (n_band, hist_tiles * 32, LANES)
    weights = (w_down, w_mid, w_up)
    early = pl.pallas_call(
        functools.partial(early_kernel, sizes),
        out_shape=(
            shaped(*hist_shape, dtype=F32),
            shaped(4, 4 * LANES, 2 * LANES),
            shaped(256, 192),
            shaped(64, 768),
            shaped(128, 576),
            shaped(128, 1024),
            shaped(16, 256),
            shaped(256, 16),
            shaped(256, 512),
            shaped(128, 576),
            shaped(256, 384),
        ),
        in_specs=[in_vmem] * 3 + [in_hbm] * 3,
        out_specs=(in_vmem,) * 11,
        scratch_shapes=[
            pltpu.SMEM((8, LANES), F32),
            vmem(n_blocks, LANES, dtype=F32),
            vmem(n_blocks, LANES, dtype=F32),
            vmem(256, 256, dtype=F32),
            vmem(32, 512, dtype=F32),
            vmem(128, 576, dtype=F32),
            vmem(64, 768, dtype=F32),
            vmem(384, 128, dtype=F32),
            vmem(640, 128, dtype=F32),
            vmem(384, 256, dtype=F32),
        ]
        + [vmem(*arg.shape) for arg in weights]
        + [pltpu.SemaphoreType.DMA((4,))],
        compiler_params=pltpu.CompilerParams(vmem_limit_bytes=16 * 1024 * 1024),
        cost_estimate=pl.CostEstimate(flops=200_000_000, bytes_accessed=2_000_000, transcendentals=700_000),
    )(packed[0], jnp.transpose(w_in, (0, 1, 3, 2)), w_head, *[in_place(arg) for arg in weights])

    _, grads, mean_tiles = pl.pallas_call(
        functools.partial(network_kernel, sizes),
        out_shape=(
            shaped(*hist_shape, dtype=F32),
            shaped(384, LANES, dtype=F32),
            shaped(n_band, own_tiles, ROWS_BAND, LANES, dtype=F32),
        ),
        in_specs=[in_vmem] * (n_band + 11),
        out_specs=(in_vmem, in_vmem, in_vmem),
        input_output_aliases={n_band: 0},
        scratch_shapes=[
            pltpu.SMEM((n_band, 8, LANES), F32),
            pltpu.SemaphoreType.DMA((n_band,)),
            vmem(rows + 2, 32, half),
            vmem(rows, 64, half, dtype=F32),
            vmem(rows + 2, 256, half),
            vmem(coarse, 32, half, dtype=F32),
            vmem(2, coarse // 2 + 2, 96, half),
            vmem(coarse, 32, half, dtype=F32),
            vmem(rows, 64, half, dtype=F32),
            vmem(rows, 64, half),
            vmem(n_band, 8, half, dtype=F32),
            vmem(n_band, 16, 2 * half),
            vmem(rows + 2, 128, half),
            vmem(rows + 2, 64, half),
            vmem(rows, 64, half),
            vmem(2, coarse // 2 + 2, 32, half),
            vmem(2, coarse // 2 + 2, 96, half),
            vmem(coarse + 2, 32, half),
            vmem(coarse + 2, 96, half),
            vmem(rows + 2, 64, half),
            vmem(n_band, n_blocks, LANES, dtype=F32),
            vmem(n_band, n_blocks, LANES, dtype=F32),
            vmem(192, 256, dtype=F32),
            vmem(96, 256, dtype=F32),
            vmem(96, 96, dtype=F32),
            vmem(32, 192, dtype=F32),
            vmem(16, 256, dtype=F32),
        ],
        compiler_params=pltpu.CompilerParams(vmem_limit_bytes=40 * 1024 * 1024),
        cost_estimate=pl.CostEstimate(flops=4_000_000_000, bytes_accessed=4_000_000, transcendentals=2_000_000),
    )(*pays, *early)

    low, high, means = reduced(grads, mean_tiles.reshape(n_band, own_tiles * ROWS_BAND, LANES), n_band, n_group)
    means = [piece.reshape(own_tiles, ROWS_BAND, LANES) for piece in means]
    outs = pl.pallas_call(
        functools.partial(unpack_kernel, (n_band, own, lon_count)),
        out_shape=(
            jax.ShapeDtypeStruct((1, ROWS_BAND, lon_count), F32),
            jax.ShapeDtypeStruct((3, 3, 8, 32), F32),
            jax.ShapeDtypeStruct((4, 4, 32, 32), F32),
            jax.ShapeDtypeStruct((3, 3, 32, 32), F32),
            jax.ShapeDtypeStruct((3, 3, 32, 64), F32),
            jax.ShapeDtypeStruct((2, 32), F32),
        ),
        in_specs=[in_vmem] * (2 + n_band),
        out_specs=(in_vmem,) * 6,
        scratch_shapes=[vmem(ROWS_BAND, n_band * own, dtype=F32)],
        compiler_params=pltpu.CompilerParams(vmem_limit_bytes=16 * 1024 * 1024),
    )(low, high, *means)
    return (outs[0], jnp.transpose(outs[1], (0, 1, 3, 2))) + tuple(outs[2:])


def solution(mesh):
    return jax.shard_map(
        local,
        mesh=mesh,
        in_specs=(
            P("group", "band", None),
            P("group", "band", None),
            P("group", "band", None),
            P("group", "band", None),
            P("group", "band", None),
            P("group", "band", None),
            P(),
            P(),
            P(),
            P(),
            P(),
            P(),
        ),
        out_specs=(P("group", "band", None), P(), P(), P(), P(), P()),
        check_vma=False,
    )
```
